256 devices in a mesh: dp: 8 (over z), tensor: 16 (over y, x), segment: 2 (over core).
Axes of the slice: x: 4, y: 4, z: 8, core: 2. Of those that a mesh axis runs over, the one named last changes fastest.
Arguments:
- x_saved: bfloat16 [2, 2, 4096, 2048], P('segment', None, 'dp', 'tensor'), may hold values from -6 to 6
- dy_in: bfloat16 [2, 4096, 2048], P(None, 'dp', 'tensor'), may hold values from -1.5 to 1.5
- w_all: bfloat16 [2, 7168, 3, 2048], P('segment', 'tensor'), may hold values from -0.125 to 0.125
- slot_token: int32 [2, 2, 2048], P('segment', None, 'dp'), may hold values from 0 to 511, as said below
- counts: int32 [2, 2, 8], P('segment', None, 'dp'), may hold values from 129 to 256, as said below
- probs: float32 [2, 2, 2048], P('segment', None, 'dp'), may hold values from 0.1 to 0.6
- adam_m: bfloat16 [2, 44040192], P('segment', ('tensor', 'dp')), may hold values from -24 to 24
- adam_v: bfloat16 [2, 44040192], P('segment', ('tensor', 'dp')), may hold values from 4 to 64
Outputs:
- dx_out: bfloat16 [2, 2, 4096, 2048], P('segment', None, 'dp', 'tensor')
- grad_sum: bfloat16 [2, 44040192], P('segment', ('tensor', 'dp'))
- new_m: bfloat16 [2, 44040192], P('segment', ('tensor', 'dp'))
- new_v: bfloat16 [2, 44040192], P('segment', ('tensor', 'dp'))
- new_w: bfloat16 [2, 44040192], P('segment', ('tensor', 'dp'))
The draws below stay inside these ranges and needn't reach their ends.
Inputs may be any that keep to these rules, and one draw needn't show every extreme that they name: `slot_token`: within each dp block of a layer and micro-batch the 256 values are distinct and ascending. `counts`: in every layer and micro-batch some dp block has all 256 rows live.
All inputs are finite; a program needn't handle non-finite values.
Results may differ from the reference program's by a relative error of at most 0.019.
Values may be sent and summed in bfloat16 or wider, within the bound.
A program may use at most 128 MiB of HBM per device.

```python
import math
import jax
import jax.numpy as jnp
from jax import lax

D = 2048
FF = 7168
MB = 2
TOK_DEV = 512
SLOTS = 256
SEGMENTS = 2
TOKENS = 4096
SLOT_ROWS = 2048
N_DP = 8
N_TENSOR = 16


def draw_slot_token(key, part):
    key = jax.random.fold_in(key, 11)
    row_keys = jax.random.split(key, SEGMENTS * MB * N_DP)

    def one_block(row_key):
        chosen = jax.random.permutation(row_key, TOK_DEV)[:SLOTS]
        return jnp.sort(chosen).astype(jnp.int32)
    values = jax.vmap(one_block)(row_keys)
    return values.reshape(SEGMENTS, MB, N_DP * SLOTS).astype(jnp.int32)


def draw_counts(key, part):
    key = jax.random.fold_in(key, 23)
    first_key, second_key = jax.random.split(key)
    drawn = jax.random.randint(first_key, (SEGMENTS, MB, N_DP), SLOTS // 2 + 1, SLOTS + 1)
    full_block = jax.random.randint(second_key, (SEGMENTS, MB, 1), 0, N_DP)
    places = jnp.arange(N_DP, dtype=jnp.int32)[None, None, :]
    return jnp.where(places == full_block, SLOTS, drawn).astype(jnp.int32)


def levels(key, dims, shards, least, high):
    gain = 1.0
    for position, blocks in shards:
        draws = jax.random.uniform(jax.random.fold_in(jax.random.fold_in(key, 6), position), (blocks,), jnp.float32, least / len(shards), high / len(shards))
        gain = gain * jnp.repeat(jnp.exp(draws), dims[position] // blocks).reshape((-1,) + (1,) * (len(dims) - 1 - position))
    return gain


def bell_draw(stream_key, shape, spread, reach, cuts=(), held_as=jnp.bfloat16):
    loudness = levels(stream_key, shape, cuts, -0.22, 0.18) if cuts else 1.0
    values = jax.random.normal(stream_key, shape, jnp.float32) * spread * loudness
    return jnp.minimum(jnp.maximum(values, -reach), reach).astype(held_as)


def setup_inputs(seed: int = 0) -> dict:
    streams_of = jax.random.split(jax.random.key(seed), 9)
    return {
        "x_saved": bell_draw(streams_of[0], (SEGMENTS, MB, TOKENS, D), 1.0, 6.0, ((0, 2), (2, 8), (3, 16))),
        "dy_in": bell_draw(streams_of[1], (MB, TOKENS, D), 0.25, 1.5, ((1, 8), (2, 16))),
        "w_all": bell_draw(streams_of[2], (SEGMENTS, FF, 3, D), D ** -0.5, 0.125, ((0, 2), (1, 16))),
        "slot_token": draw_slot_token(jax.random.fold_in(streams_of[8], 71), 0),
        "counts": draw_counts(jax.random.fold_in(streams_of[8], 71), 0),
        "probs": jnp.clip(0.1 + 0.5 * jax.random.uniform(streams_of[5], (SEGMENTS, MB, SLOT_ROWS), jnp.float32) ** levels(streams_of[5], (SEGMENTS, MB, SLOT_ROWS), ((0, 2), (2, 8)), -0.2, 0.2), 0.1, 0.6),
        "adam_m": bell_draw(streams_of[6], (SEGMENTS, 3 * FF * D), 4.0, 24.0, ((0, 2), (1, 128))),
        "adam_v": jnp.clip(jnp.exp(math.log(64.0) - 2.7725887 * jax.random.uniform(streams_of[7], (SEGMENTS, 3 * FF * D), jnp.float32) ** levels(streams_of[7], (SEGMENTS, 3 * FF * D), ((0, 2), (1, 128)), -0.2, 0.2)), 4.0, 64.0).astype(jnp.bfloat16),
    }


beta_one = 0.9
beta_two = 0.95
learning_rate = 0.01
adam_epsilon = 1e-08
bias_one = 0.9999734386011124
bias_two = 0.994079470779666

def rounded(value):
    return lax.optimization_barrier(value.astype(jnp.bfloat16)).astype(jnp.float32)

def expert_rows(inputs, grads, weights):
    gate_pre = jnp.dot(inputs, weights[:, 0, :].T, preferred_element_type=jnp.float32)
    up_pre = jnp.dot(inputs, weights[:, 1, :].T, preferred_element_type=jnp.float32)
    sigmoid_g = jax.nn.sigmoid(gate_pre)
    active = gate_pre * sigmoid_g
    hidden = (active * up_pre).astype(jnp.bfloat16)
    hidden_grad = jnp.dot(grads, weights[:, 2, :].T, preferred_element_type=jnp.float32)
    d_gate = (hidden_grad * up_pre * sigmoid_g * (1.0 + gate_pre * (1.0 - sigmoid_g))).astype(jnp.bfloat16)
    d_up = (hidden_grad * active).astype(jnp.bfloat16)
    return (hidden, d_gate, d_up)

def reference(x_saved, dy_in, w_all, slot_token, counts, probs, adam_m, adam_v):
    hidden_dev = FF // N_TENSOR
    row_ids = jnp.arange(SLOT_ROWS, dtype=jnp.int32)
    base_ids = row_ids // SLOTS * TOK_DEV
    upstream = dy_in
    dx_list = [None] * SEGMENTS
    grad_list = [None] * SEGMENTS
    m_list = [None] * SEGMENTS
    v_list = [None] * SEGMENTS
    w_list = [None] * SEGMENTS
    for segment_no in range(SEGMENTS - 1, -1, -1):
        weights = w_all[segment_no]
        stored = []
        dx_segment = []
        for micro_no in range(MB):
            token_ids = (slot_token[segment_no, micro_no] + base_ids).astype(jnp.int32)
            live = row_ids % SLOTS < jnp.repeat(counts[segment_no, micro_no], SLOTS)
            inputs = x_saved[segment_no, micro_no][token_ids]
            gating = jnp.where(live, probs[segment_no, micro_no], 0.0)
            grads = (gating[:, None] * upstream[micro_no][token_ids].astype(jnp.float32)).astype(jnp.bfloat16)
            hidden, d_gate, d_up = expert_rows(inputs, grads, weights)
            summed = jnp.zeros((SLOT_ROWS, D), jnp.float32)
            for group in range(N_TENSOR):
                lower = group * hidden_dev
                upper = lower + hidden_dev
                term = jnp.dot(d_gate[:, lower:upper], weights[lower:upper, 0, :], preferred_element_type=jnp.float32)
                term = term + jnp.dot(d_up[:, lower:upper], weights[lower:upper, 1, :], preferred_element_type=jnp.float32)
                summed = summed + rounded(term)
            result = upstream[micro_no].astype(jnp.float32).at[token_ids].add(summed)
            dx_segment.append(result.astype(jnp.bfloat16))
            stored.append((inputs, grads, hidden, d_gate, d_up))
        upstream = jnp.stack(dx_segment)
        dx_list[segment_no] = upstream

        def block_grad(block_no):
            lower = block_no * SLOTS
            upper = lower + SLOTS
            inputs = jnp.concatenate([item[0][lower:upper] for item in stored], 0)
            grads = jnp.concatenate([item[1][lower:upper] for item in stored], 0)
            hidden = jnp.concatenate([item[2][lower:upper] for item in stored], 0)
            d_gate = jnp.concatenate([item[3][lower:upper] for item in stored], 0)
            d_up = jnp.concatenate([item[4][lower:upper] for item in stored], 0)
            gate_grad = jnp.dot(d_gate.T, inputs, preferred_element_type=jnp.float32)
            up_grad = jnp.dot(d_up.T, inputs, preferred_element_type=jnp.float32)
            down_grad = jnp.dot(hidden.T, grads, preferred_element_type=jnp.float32)
            return jnp.stack([gate_grad, up_grad, down_grad], axis=1)
        reduced = jnp.zeros((FF, 3, D), jnp.float32)
        for block_no in range(N_DP):
            reduced = reduced + rounded(block_grad(block_no))
        grad_flat = reduced.astype(jnp.bfloat16).reshape(-1)
        grad_value = grad_flat.astype(jnp.float32)
        moment_one = beta_one * adam_m[segment_no].astype(jnp.float32) + (1.0 - beta_one) * grad_value
        moment_two = beta_two * adam_v[segment_no].astype(jnp.float32) + (1.0 - beta_two) * grad_value * grad_value
        update = moment_one / bias_one / (jnp.sqrt(moment_two / bias_two) + adam_epsilon)
        new_weight = weights.reshape(-1).astype(jnp.float32) - learning_rate * update
        grad_list[segment_no] = grad_flat
        m_list[segment_no] = moment_one.astype(jnp.bfloat16)
        v_list[segment_no] = moment_two.astype(jnp.bfloat16)
        w_list[segment_no] = new_weight.astype(jnp.bfloat16)
    return (jnp.stack(dx_list), jnp.stack(grad_list), jnp.stack(m_list), jnp.stack(v_list), jnp.stack(w_list))
```

```python
import functools

import jax
import jax.numpy as jnp
from jax import lax
from jax.experimental import pallas as pl
from jax.experimental.pallas import tpu as pltpu
from jax.sharding import PartitionSpec as P

beta_one = 0.9
beta_two = 0.95
learning_rate = 0.01
adam_epsilon = 1e-08
bias_one = 0.9999734386011124
bias_two = 0.994079470779666

MESH = pl.DeviceIdType.MESH
BF = jnp.bfloat16
F32 = jnp.float32
N_DP = 8
N_TENSOR = 16
WIDE = 128
D = N_TENSOR * WIDE
ROWS = 256
TOK = 512
HID = 448
PAD = 512
PIECE = HID // N_DP
HALF = D // 2
QUAR = D // 4
STACK = 2 * PIECE


def dot(left, right, left_dim, right_dim):
    return lax.dot_general(
        left, right, (((left_dim,), (right_dim,)), ((), ())), preferred_element_type=F32
    )


def kernel(x_ref, dy_ref, pick_ref, gate_ref, w_ref, dx_ref, g_ref,
           w, picks, gates, xr, xd, act, coef, hid, dg, du, trans, back, rs,
           gsend, gown, grecv, first, ring, gsum, goth, dxs, dxoth, upd,
           own_sem, w_sem, pg_sem, xr_sem, ag_send, ag_recv, rs_send, rs_recv,
           gx_sem, first_sem, ring_send, ring_recv, gs_sem, dx_sem):
    me_d, me_t, me_c = lax.axis_index("dp"), lax.axis_index("tensor"), lax.axis_index("segment")
    other = 1 - me_c
    my_cols = pl.ds(pl.multiple_of(me_t * WIDE, WIDE), WIDE)

    def at_tensor(n):
        return (me_d, n, me_c)

    def at_dp(n):
        return (n, me_t, me_c)

    partner = (me_d, me_t, other)
    up_d, down_d = lax.rem(me_d + 1, N_DP), lax.rem(me_d + N_DP - 1, N_DP)

    def peer(k):
        return ((me_t // 4 + k // 4) % 4) * 4 + (me_t % 4 + k % 4) % 4

    barrier = pltpu.get_barrier_semaphore()

    def greet(k, carry):
        pl.semaphore_signal(barrier, inc=1, device_id=at_tensor(peer(k)), device_id_type=MESH)
        return carry
    lax.fori_loop(1, N_TENSOR, greet, 0)
    pl.semaphore_signal(barrier, inc=1, device_id=partner, device_id_type=MESH)
    pl.semaphore_signal(barrier, inc=1, device_id=at_dp(up_d), device_id_type=MESH)
    pl.semaphore_signal(barrier, inc=1, device_id=at_dp(down_d), device_id_type=MESH)

    own_w = pltpu.make_async_copy(w_ref, w.at[me_c, :, pl.ds(0, HID)], own_sem.at[0])
    own_w.start()
    for layer in range(2):
        for kind in range(3):
            w[layer, kind, HID:PAD, :] = jnp.zeros((PAD - HID, D), BF)
    picks[me_c] = pick_ref[me_c]
    gates[me_c] = gate_ref[me_c]

    def rows_of(micro):
        choice = pick_ref[micro]
        picked = dot(choice, x_ref[micro], 1, 0)
        grads = gate_ref[micro] * dot(choice, dy_ref[micro], 1, 0)
        return picked.astype(BF), grads.astype(BF)

    there = rows_of(other)
    xr[2, 0] = there[0]
    xr[2, 1] = there[1]
    here = rows_of(me_c)
    xr[me_c, 0] = here[0]
    xr[me_c, 1] = here[1]

    pl.semaphore_wait(barrier, N_TENSOR + 2)

    def to_partner(src, dst, sems, index=None):
        send = sems.at[0] if index is None else sems.at[0, index]
        recv = sems.at[1] if index is None else sems.at[1, index]
        return pltpu.make_async_remote_copy(
            src_ref=src, dst_ref=dst, send_sem=send, recv_sem=recv,
            device_id=partner, device_id_type=MESH)

    xr_copy = to_partner(xr.at[2], xr.at[me_c], xr_sem)
    xr_copy.start()
    w_copy = to_partner(w_ref, w.at[me_c, :, pl.ds(0, HID)], w_sem)
    w_copy.start()
    pick_copy = to_partner(pick_ref.at[other], picks.at[me_c], pg_sem, 0)
    pick_copy.start()
    gate_copy = to_partner(gate_ref.at[other], gates.at[me_c], pg_sem, 1)
    gate_copy.start()

    def gather_copy(src, dst, use, n, owner):
        columns = pl.ds(pl.multiple_of(owner * WIDE, WIDE), WIDE)
        return pltpu.make_async_remote_copy(
            src_ref=src, dst_ref=dst(columns), send_sem=ag_send.at[use, n],
            recv_sem=ag_recv.at[use, owner], device_id=at_tensor(n), device_id_type=MESH)

    def gather_start(src, dst, use):
        def step(k, carry):
            gather_copy(src, dst, use, peer(k), me_t).start()
            return carry
        lax.fori_loop(1, N_TENSOR, step, 0)

    def gather_wait(src, dst, use):
        def step(k, carry):
            n = peer(k)
            gather_copy(src, dst, use, n, n).wait_recv()
            gather_copy(src, dst, use, n, me_t).wait_send()
            return carry
        lax.fori_loop(1, N_TENSOR, step, 0)

    def both_of_one(columns):
        return xd.at[1, :, :, columns]

    def inputs_of_zero(columns):
        return xd.at[0, 0, :, columns]

    def grads_of_zero(columns):
        return xd.at[0, 1, :, columns]

    xr_copy.wait()
    gather_start(xr.at[1], both_of_one, 0)
    gather_start(xr.at[0, 0], inputs_of_zero, 1)
    for kind in range(2):
        xd[1, kind, :, my_cols] = xr[1, kind]
    xd[0, 0, :, my_cols] = xr[0, 0]
    own_w.wait()
    w_copy.wait()
    pick_copy.wait()
    gate_copy.wait()

    def forward(layer):
        def step(block, carry):
            span = pl.ds(pl.multiple_of(block * 256, 256), 256)
            inputs = xd[layer, 0]
            gate_pre = dot(inputs, w[layer, 0, span, :], 1, 1)
            up_pre = dot(inputs, w[layer, 1, span, :], 1, 1)
            sig = 1.0 / (1.0 + jnp.exp(-gate_pre))
            active = gate_pre * sig
            act[:, span] = active
            coef[:, span] = up_pre * sig * (1.0 + gate_pre * (1.0 - sig))
            hid[:, span] = (active * up_pre).astype(BF)
            return carry
        lax.fori_loop(0, PAD // 256, step, 0)

    def hidden_grads(layer):
        def step(block, carry):
            span = pl.ds(pl.multiple_of(block * 256, 256), 256)
            grad = dot(xd[layer, 1], w[layer, 2, span, :], 1, 1)
            dg[:, span] = (grad * coef[:, span]).astype(BF)
            du[:, span] = (grad * act[:, span]).astype(BF)
            return carry
        lax.fori_loop(0, PAD // 256, step, 0)

    def scatter_copy(layer, n, owner):
        return pltpu.make_async_remote_copy(
            src_ref=back.at[layer, n], dst_ref=rs.at[layer, owner],
            send_sem=rs_send.at[layer, n], recv_sem=rs_recv.at[layer, owner],
            device_id=at_tensor(n), device_id_type=MESH)

    def row_grads(layer):
        def step(index, carry):
            pair = lax.rem(me_t // 2 + 1 + index, N_TENSOR // 2)
            span = pl.ds(pl.multiple_of(pair * 256, 256), 256)
            term = dot(dg[...], w[layer, 0, :, span], 1, 0)
            term = (term + dot(du[...], w[layer, 1, :, span], 1, 0)).astype(BF)
            for side in range(2):
                n = pair * 2 + side
                back[layer, n] = term[:, side * WIDE:(side + 1) * WIDE]

                @pl.when(n != me_t)
                def _():
                    scatter_copy(layer, n, me_t).start()
            return carry
        lax.fori_loop(0, N_TENSOR // 2, step, 0)

    def summed_rows(layer):
        def step(k, total):
            n = peer(k)
            scatter_copy(layer, n, n).wait_recv()
            scatter_copy(layer, n, me_t).wait_send()
            return total + rs[layer, n].astype(F32)
        return lax.fori_loop(1, N_TENSOR, step, back[layer, me_t].astype(F32))

    def to_tokens(layer, upstream):
        total = summed_rows(layer)
        high = total.astype(BF)
        low = (total - high.astype(F32)).astype(BF)
        spread = dot(picks[layer], high, 0, 0) + dot(picks[layer], low, 0, 0)
        dxs[layer] = (upstream.astype(F32) + spread).astype(BF)

    def weight_half(layer, half, dst, send):
        def step(kind, carry):
            parts = []
            for quarter in range(2):
                span = pl.ds(pl.multiple_of(half * HALF + quarter * QUAR, QUAR), QUAR)
                parts.append(dot(trans[kind], xd[layer, kind // 2, :, span], 1, 0))
            for d in range(N_DP):
                rows = slice(d * PIECE, (d + 1) * PIECE)
                both = jnp.concatenate([parts[0][rows], parts[1][rows]], axis=0)
                dst[layer, kind, d] = both.astype(BF)
            if send:
                pair_copy(layer, kind).start()
            return carry
        lax.fori_loop(0, 3, step, 0)

    def pair_copy(layer, kind):
        return pltpu.make_async_remote_copy(
            src_ref=gsend.at[layer, kind], dst_ref=grecv.at[layer, kind],
            send_sem=gx_sem.at[0, layer, kind], recv_sem=gx_sem.at[1, layer, kind],
            device_id=partner, device_id_type=MESH)

    def weight_grads_away(layer):
        trans[0] = dg[...].T
        trans[1] = du[...].T
        trans[2] = hid[...].T
        weight_half(layer, other, gsend, True)

    def weight_grads_here(layer):
        weight_half(layer, me_c, gown, False)

    sides = ((up_d, 1), (down_d, -1))

    def mine(layer, kind, d):
        return gown[layer, kind, d].astype(F32) + grecv[layer, kind, d].astype(F32)

    def first_copy(layer, kind, way):
        columns = slice(way * 256, (way + 1) * 256)
        return pltpu.make_async_remote_copy(
            src_ref=first.at[layer, way, kind],
            dst_ref=ring.at[layer, way, 0, kind, :, columns],
            send_sem=first_sem.at[layer, way, kind], recv_sem=ring_recv.at[layer, way, 0, kind],
            device_id=at_dp(sides[way][0]), device_id_type=MESH)

    def ring_copy(layer, kind, way, step):
        return pltpu.make_async_remote_copy(
            src_ref=ring.at[layer, way, step - 1, kind], dst_ref=ring.at[layer, way, step, kind],
            send_sem=ring_send.at[layer, way, step - 1, kind],
            recv_sem=ring_recv.at[layer, way, step, kind],
            device_id=at_dp(sides[way][0]), device_id_type=MESH)

    def ring_first(layer):
        far = lax.rem(me_d + N_DP // 2, N_DP)

        def step(kind, carry):
            pair_copy(layer, kind).wait()
            value = mine(layer, kind, far).astype(BF)
            for way in range(2):
                first[layer, way, kind] = value[:, way * 256:(way + 1) * 256]
                first_copy(layer, kind, way).start()
            return carry
        lax.fori_loop(0, 3, step, 0)

    def ring_step(layer, number):
        def step(kind, carry):
            for way in range(2):
                target = lax.rem(me_d + N_DP + (4 - number) * sides[way][1], N_DP)
                value = mine(layer, kind, target)
                slot = ring.at[layer, way, number - 1, kind]
                if number == 1:
                    first_copy(layer, kind, way).wait()
                    columns = slice(way * 256, (way + 1) * 256)
                    rest = slice((1 - way) * 256, (2 - way) * 256)
                    slot[:, columns] = (slot[:, columns].astype(F32) + value[:, columns]).astype(BF)
                    slot[:, rest] = value[:, rest].astype(BF)
                else:
                    ring_copy(layer, kind, way, number - 1).wait()
                    slot[...] = (slot[...].astype(F32) + value).astype(BF)
                ring_copy(layer, kind, way, number).start()
            return carry
        lax.fori_loop(0, 3, step, 0)

    def ring_last(layer):
        def step(kind, carry):
            value = mine(layer, kind, me_d)
            for way in range(2):
                ring_copy(layer, kind, way, 3).wait()
                value = value + ring[layer, way, 3, kind].astype(F32)
            gsum[layer, kind] = value.astype(BF)
            return carry
        lax.fori_loop(0, 3, step, 0)

    gather_wait(xr.at[1], both_of_one, 0)
    forward(1)
    hidden_grads(1)
    row_grads(1)
    weight_grads_away(1)
    weight_grads_here(1)
    ring_first(1)
    gather_wait(xr.at[0, 0], inputs_of_zero, 1)
    forward(0)
    to_tokens(1, dy_ref[me_c])
    upd[...] = (gates[0] * dot(picks[0], dxs[1], 1, 0)).astype(BF)
    gather_start(upd, grads_of_zero, 2)
    xd[0, 1, :, my_cols] = upd[...]
    ring_step(1, 1)
    gather_wait(upd, grads_of_zero, 2)
    hidden_grads(0)
    row_grads(0)
    ring_step(1, 2)
    weight_grads_away(0)
    weight_grads_here(0)
    ring_step(1, 3)
    ring_first(0)
    to_tokens(0, dxs[1])
    dx_copy = to_partner(dxs.at[other], dxoth, dx_sem)
    dx_copy.start()
    ring_last(1)
    ring_step(0, 1)
    ring_step(0, 2)
    ring_step(0, 3)
    dx_copy.wait()
    dx_ref[me_c] = dxs[me_c]
    dx_ref[other] = dxoth[...]
    ring_last(0)
    sum_copy = to_partner(gsum.at[other], goth, gs_sem)
    sum_copy.start()
    g_ref[me_c] = gsum[me_c]
    sum_copy.wait()
    g_ref[other] = goth[...]


def backward(saved, dy, pick, gating, weights):
    dma = pltpu.SemaphoreType.DMA
    vmem = pl.BlockSpec(memory_space=pltpu.VMEM)
    scratch = [
        pltpu.VMEM((2, 3, PAD, D), BF),
        pltpu.VMEM((2, ROWS, TOK), BF),
        pltpu.VMEM((2, ROWS, WIDE), F32),
        pltpu.VMEM((3, 2, ROWS, WIDE), BF),
        pltpu.VMEM((2, 2, ROWS, D), BF),
        pltpu.VMEM((ROWS, PAD), F32),
        pltpu.VMEM((ROWS, PAD), F32),
        pltpu.VMEM((ROWS, PAD), BF),
        pltpu.VMEM((ROWS, PAD), BF),
        pltpu.VMEM((ROWS, PAD), BF),
        pltpu.VMEM((3, PAD, ROWS), BF),
        pltpu.VMEM((2, N_TENSOR, ROWS, WIDE), BF),
        pltpu.VMEM((2, N_TENSOR, ROWS, WIDE), BF),
        pltpu.VMEM((2, 3, N_DP, STACK, QUAR), BF),
        pltpu.VMEM((2, 3, N_DP, STACK, QUAR), BF),
        pltpu.VMEM((2, 3, N_DP, STACK, QUAR), BF),
        pltpu.VMEM((2, 2, 3, STACK, QUAR // 2), BF),
        pltpu.VMEM((2, 2, 4, 3, STACK, QUAR), BF),
        pltpu.VMEM((2, 3, STACK, QUAR), BF),
        pltpu.VMEM((3, STACK, QUAR), BF),
        pltpu.VMEM((2, TOK, WIDE), BF),
        pltpu.VMEM((TOK, WIDE), BF),
        pltpu.VMEM((ROWS, WIDE), BF),
        dma((1,)), dma((2,)), dma((2, 2)), dma((2,)),
        dma((3, N_TENSOR)), dma((3, N_TENSOR)), dma((2, N_TENSOR)), dma((2, N_TENSOR)),
        dma((2, 2, 3)), dma((2, 2, 3)), dma((2, 2, 3, 3)), dma((2, 2, 4, 3)), dma((2,)), dma((2,)),
    ]
    return pl.pallas_call(
        kernel,
        out_shape=(
            jax.ShapeDtypeStruct((2, TOK, WIDE), BF),
            jax.ShapeDtypeStruct((2, 3, STACK, QUAR), BF),
        ),
        in_specs=[vmem, vmem, vmem, vmem, pl.BlockSpec(memory_space=pl.ANY)],
        out_specs=(vmem, vmem),
        scratch_shapes=scratch,
        compiler_params=pltpu.CompilerParams(
            collective_id=0, has_side_effects=True, vmem_limit_bytes=60 * 2**20),
        cost_estimate=pl.CostEstimate(
            flops=16 * 2 * ROWS * HID * D, bytes_accessed=30 * 2**20, transcendentals=2 * ROWS * HID),
    )(saved, dy, pick, gating, weights)


def local(x_saved, dy_in, w_all, slot_token, counts, probs, adam_m, adam_v):
    weights = jnp.transpose(w_all[0], (1, 0, 2))
    tokens = jnp.arange(TOK, dtype=jnp.int32)
    pick = (slot_token[0][:, :, None] == tokens).astype(BF)
    positions = jnp.arange(ROWS, dtype=jnp.int32)
    live = positions[None, :] < counts[0]
    gating = jnp.broadcast_to(jnp.where(live, probs[0], 0.0)[:, :, None], (2, ROWS, WIDE))
    results, sums = backward(x_saved[0], dy_in, pick, gating, weights)
    grad_piece = jnp.transpose(sums.reshape(2, 3, 2, PIECE, QUAR), (3, 1, 0, 2, 4)).reshape(-1)
    grad_value = grad_piece.astype(F32)
    moment_one = beta_one * adam_m[0].astype(F32) + (1.0 - beta_one) * grad_value
    moment_two = beta_two * adam_v[0].astype(F32) + (1.0 - beta_two) * grad_value * grad_value
    own = lax.dynamic_slice_in_dim(w_all[0], lax.axis_index("dp") * PIECE, PIECE, 0)
    own_weights = own.reshape(-1).astype(F32)
    update = moment_one / bias_one / (jnp.sqrt(moment_two / bias_two) + adam_epsilon)
    new_weight = own_weights - learning_rate * update
    return (
        results[None],
        grad_piece[None],
        moment_one.astype(BF)[None],
        moment_two.astype(BF)[None],
        new_weight.astype(BF)[None],
    )


def solution(mesh):
    return jax.shard_map(
        local,
        mesh=mesh,
        in_specs=(
            P("segment", None, "dp", "tensor"),
            P(None, "dp", "tensor"),
            P("segment", "tensor", None, None),
            P("segment", None, "dp"),
            P("segment", None, "dp"),
            P("segment", None, "dp"),
            P("segment", ("tensor", "dp")),
            P("segment", ("tensor", "dp")),
        ),
        out_specs=(
            P("segment", None, "dp", "tensor"),
            P("segment", ("tensor", "dp")),
            P("segment", ("tensor", "dp")),
            P("segment", ("tensor", "dp")),
            P("segment", ("tensor", "dp")),
        ),
        check_vma=False,
    )
```

```python
import functools

import jax
import jax.numpy as jnp
from jax import lax
from jax.experimental import pallas as pl
from jax.experimental.pallas import tpu as pltpu
from jax.sharding import PartitionSpec as P

beta_one = 0.9
beta_two = 0.95
learning_rate = 0.01
adam_epsilon = 1e-08
bias_one = 0.9999734386011124
bias_two = 0.994079470779666

MESH = pl.DeviceIdType.MESH
BF = jnp.bfloat16
F32 = jnp.float32
N_DP = 8
N_TENSOR = 16
WIDE = 128
D = N_TENSOR * WIDE
ROWS = 256
TOK = 512
HID = 448
PAD = 512
PIECE = HID // N_DP
HALF = D // 2
QUAR = D // 4
STACK = 2 * PIECE
SHARE = 3 * PIECE * D
CHUNK = 8192
STEPS = 6


def dot(left, right, left_dim, right_dim):
    return lax.dot_general(
        left, right, (((left_dim,), (right_dim,)), ((), ())), preferred_element_type=F32
    )


def kernel(x_ref, dy_ref, slot_ref, count_ref, prob_ref, w_ref,
           dx_ref, g_ref, w_out_ref,
           w, picks, gates, xr, xd, act, coef, hid, dg, du, trans, back, rs,
           gsend, gown, grecv, first, ring, gsum, goth, dxs, dxoth, upd,
           flat_g, flat_w, window,
           own_sem, w_sem, pg_sem, xr_sem, ag_send, ag_recv, rs_send, rs_recv,
           gx_sem, first_sem, ring_send, ring_recv, gs_sem, dx_sem):
    me_d, me_t, me_c = lax.axis_index("dp"), lax.axis_index("tensor"), lax.axis_index("segment")
    other = 1 - me_c
    my_y, my_x = me_t // 4, lax.rem(me_t, 4)

    def at_tensor(n):
        return (me_d, n, me_c)

    def at_dp(n):
        return (n, me_t, me_c)

    partner = (me_d, me_t, other)
    up_d, down_d = lax.rem(me_d + 1, N_DP), lax.rem(me_d + N_DP - 1, N_DP)

    def peer(k):
        return ((me_t // 4 + k // 4) % 4) * 4 + (me_t % 4 + k % 4) % 4

    barrier = pltpu.get_barrier_semaphore()

    def greet(k, carry):
        pl.semaphore_signal(barrier, inc=1, device_id=at_tensor(peer(k)), device_id_type=MESH)
        return carry
    lax.fori_loop(1, N_TENSOR, greet, 0)
    pl.semaphore_signal(barrier, inc=1, device_id=partner, device_id_type=MESH)
    pl.semaphore_signal(barrier, inc=1, device_id=at_dp(up_d), device_id_type=MESH)
    pl.semaphore_signal(barrier, inc=1, device_id=at_dp(down_d), device_id_type=MESH)

    own_w = pltpu.make_async_copy(w_ref, w.at[me_c, :, pl.ds(0, HID)], own_sem.at[0])
    own_w.start()
    for layer in range(2):
        for kind in range(3):
            w[layer, kind, HID:PAD, :] = jnp.zeros((PAD - HID, D), BF)
    def rows_of(micro, slot):
        chosen = slot_ref[pl.ds(micro, 1), :]
        tokens = lax.broadcasted_iota(jnp.int32, (TOK, ROWS), 0)
        onehot = jnp.where(tokens == chosen, 1.0, 0.0)
        picks[slot] = onehot.astype(BF)
        both_counts = count_ref[...]
        at_micro = lax.broadcasted_iota(jnp.int32, both_counts.shape, 1) == micro
        count = jnp.sum(jnp.where(at_micro, both_counts, 0), axis=1, keepdims=True)
        live = lax.broadcasted_iota(jnp.int32, (1, ROWS), 1) < count
        gating = jnp.where(live, prob_ref[pl.ds(micro, 1), :], 0.0)
        scale = jnp.broadcast_to(gating, (WIDE, ROWS)).T
        gates[slot] = scale
        both = jnp.concatenate([x_ref[micro], dy_ref[micro]], axis=1)
        picked = dot(picks[slot], both, 0, 0)
        xr[slot, 0] = picked[:, :WIDE].astype(BF)
        xr[slot, 1] = (scale * picked[:, WIDE:]).astype(BF)

    rows_of(other, 2)
    rows_of(me_c, me_c)

    pl.semaphore_wait(barrier, N_TENSOR + 2)

    def to_partner(src, dst, sems, index=None):
        send = sems.at[0] if index is None else sems.at[0, index]
        recv = sems.at[1] if index is None else sems.at[1, index]
        return pltpu.make_async_remote_copy(
            src_ref=src, dst_ref=dst, send_sem=send, recv_sem=recv,
            device_id=partner, device_id_type=MESH)

    xr_copy = to_partner(xr.at[2], xr.at[me_c], xr_sem)
    xr_copy.start()
    w_copy = to_partner(w_ref, w.at[me_c, :, pl.ds(0, HID)], w_sem)
    w_copy.start()
    pick_copy = to_partner(picks.at[2], picks.at[me_c], pg_sem, 0)
    pick_copy.start()
    gate_copy = to_partner(gates.at[2], gates.at[me_c], pg_sem, 1)
    gate_copy.start()

    def hop(use, phase, which, ref, device):
        return pltpu.make_async_remote_copy(
            src_ref=ref, dst_ref=ref, send_sem=ag_send.at[use, phase, which],
            recv_sem=ag_recv.at[use, phase, which], device_id=device, device_id_type=MESH)

    class Piece:
        def __init__(self, use, layer, kind, start, rows, x_first, direct):
            self.use, self.layer, self.kind = use, layer, kind
            self.start, self.rows, self.x_first, self.direct = start, rows, x_first, direct

        def at(self, phase, shift):
            if self.x_first == (phase == 0):
                return at_tensor(my_y * 4 + (my_x + shift) % 4)
            return at_tensor((my_y + shift) % 4 * 4 + my_x)

        def block(self, phase, shift, part):
            along_x = self.x_first == (phase == 0)
            low, count = {"all": (0, self.rows), "low": (0, self.rows // 2),
                          "high": (self.rows // 2, self.rows // 2)}[part]
            rows = slice(self.start + low, self.start + low + count)
            index = ((my_x if along_x else my_y) + shift) % 4
            columns = pl.ds(pl.multiple_of((index if along_x else my_x) * WIDE, WIDE), WIDE)
            array = xd.at[self.layer] if self.kind is None else xd.at[self.layer, pl.ds(self.kind, 1)]
            if phase == 0:
                return array.at[:, my_y if along_x else index, rows, columns]
            return array.at[:, :, rows, columns] if along_x else array.at[:, index, rows, :]

        def put(self, values):
            columns = pl.ds(pl.multiple_of(my_x * WIDE, WIDE), WIDE)
            first = 0 if self.kind is None else self.kind
            for index, value in enumerate(values):
                rows = slice(self.start, self.start + self.rows)
                xd[self.layer, first + index, my_y, rows, columns] = value[rows]

        def hops(self, phase):
            own = [(0, 1, "all", 0, 3), (1, 3, "all", 0, 1)]
            if self.direct:
                return own + [(2, 2, "all", 0, 2)], []
            return own, [(2, 1, "low", 3, 2), (3, 3, "high", 1, 2)]

        def copy(self, phase, hop_of, owner):
            which, shift, part, _, _ = hop_of
            return hop(self.use, phase, which, self.block(phase, owner, part), self.at(phase, shift))

        def send(self, phase):
            if phase == 1:
                self.finish(0)
            for one in self.hops(phase)[0]:
                self.copy(phase, one, one[3]).start()

        def forward(self, phase):
            own, later = self.hops(phase)
            for one, two in zip(own, later):
                self.copy(phase, one, one[4]).wait_recv()
                self.copy(phase, two, two[3]).start()

        def finish(self, phase):
            own, later = self.hops(phase)
            for one in later or own:
                self.copy(phase, one, one[4]).wait_recv()

        def drain(self):
            for phase in range(2):
                own, later = self.hops(phase)
                for one in own + later:
                    self.copy(phase, one, one[3]).wait_send()

    part = ROWS // 2

    def pieces_of(use, layer, kind, direct):
        return (Piece(use, layer, kind, 0, part, True, direct),
                Piece(use + 1, layer, kind, part, part, False, direct))

    ones = pieces_of(0, 1, None, True)
    zeros = pieces_of(2, 0, 0, True)
    grads = pieces_of(4, 0, 1, True)

    def launch(pieces, values):
        for piece in pieces:
            piece.put(values)
            piece.send(0)

    xr_copy.wait()
    launch(ones, (xr[1, 0], xr[1, 1]))
    for piece in ones:
        piece.forward(0)
    for piece in ones:
        piece.send(1)
    launch(zeros, (xr[0, 0],))
    for piece in ones:
        piece.forward(1)
    for piece in zeros:
        piece.forward(0)
    for piece in zeros:
        piece.send(1)
    own_w.wait()
    w_copy.wait()
    pick_copy.wait()
    gate_copy.wait()

    def wide_dot(layer, kind, matrix, span):
        total = None
        for y in range(4):
            part = dot(xd[layer, kind, y], w[layer, matrix, span, y * QUAR:(y + 1) * QUAR], 1, 1)
            total = part if total is None else total + part
        return total

    def forward(layer):
        def step(block, carry):
            span = pl.ds(pl.multiple_of(block * 256, 256), 256)
            gate_pre = wide_dot(layer, 0, 0, span)
            up_pre = wide_dot(layer, 0, 1, span)
            sig = 1.0 / (1.0 + jnp.exp(-gate_pre))
            active = gate_pre * sig
            act[:, span] = active
            coef[:, span] = up_pre * sig * (1.0 + gate_pre * (1.0 - sig))
            hid[:, span] = (active * up_pre).astype(BF)
            return carry
        lax.fori_loop(0, PAD // 256, step, 0)

    def hidden_grads(layer):
        def step(block, carry):
            span = pl.ds(pl.multiple_of(block * 256, 256), 256)
            grad = wide_dot(layer, 1, 2, span)
            dg[:, span] = (grad * coef[:, span]).astype(BF)
            du[:, span] = (grad * act[:, span]).astype(BF)
            return carry
        lax.fori_loop(0, PAD // 256, step, 0)

    def scatter_copy(layer, n, owner):
        return pltpu.make_async_remote_copy(
            src_ref=back.at[layer, n], dst_ref=rs.at[layer, owner],
            send_sem=rs_send.at[layer, n], recv_sem=rs_recv.at[layer, owner],
            device_id=at_tensor(n), device_id_type=MESH)

    def row_grads(layer):
        def step(index, carry):
            pair = lax.rem(me_t // 2 + 1 + index, N_TENSOR // 2)
            span = pl.ds(pl.multiple_of(pair * 256, 256), 256)
            term = dot(dg[...], w[layer, 0, :, span], 1, 0)
            term = (term + dot(du[...], w[layer, 1, :, span], 1, 0)).astype(BF)
            for side in range(2):
                n = pair * 2 + side
                back[layer, n] = term[:, side * WIDE:(side + 1) * WIDE]

                @pl.when(n != me_t)
                def _():
                    scatter_copy(layer, n, me_t).start()
            return carry
        lax.fori_loop(0, N_TENSOR // 2, step, 0)

    def summed_rows(layer):
        def step(k, total):
            n = peer(k)
            scatter_copy(layer, n, n).wait_recv()
            scatter_copy(layer, n, me_t).wait_send()
            return total + rs[layer, n].astype(F32)
        return lax.fori_loop(1, N_TENSOR, step, back[layer, me_t].astype(F32))

    def to_tokens(layer, upstream):
        total = summed_rows(layer)
        high = total.astype(BF)
        low = (total - high.astype(F32)).astype(BF)
        spread = dot(picks[layer], high, 1, 0) + dot(picks[layer], low, 1, 0)
        dxs[layer] = (upstream.astype(F32) + spread).astype(BF)

    def weight_half(layer, half, dst, send):
        def step(kind, carry):
            parts = []
            for quarter in range(2):
                parts.append(dot(trans[kind], xd[layer, kind // 2, half * 2 + quarter], 1, 0))
            for d in range(N_DP):
                rows = slice(d * PIECE, (d + 1) * PIECE)
                both = jnp.concatenate([parts[0][rows], parts[1][rows]], axis=0)
                dst[layer, kind, d] = both.astype(BF)
            if send:
                pair_copy(layer, kind).start()
            return carry
        lax.fori_loop(0, 3, step, 0)

    def pair_copy(layer, kind):
        return pltpu.make_async_remote_copy(
            src_ref=gsend.at[layer, kind], dst_ref=grecv.at[layer, kind],
            send_sem=gx_sem.at[0, layer, kind], recv_sem=gx_sem.at[1, layer, kind],
            device_id=partner, device_id_type=MESH)

    def weight_grads_away(layer):
        trans[0] = dg[...].T
        trans[1] = du[...].T
        trans[2] = hid[...].T
        weight_half(layer, other, gsend, True)

    def weight_grads_here(layer):
        weight_half(layer, me_c, gown, False)

    sides = ((up_d, 1), (down_d, -1))

    def mine(layer, kind, d):
        return gown[layer, kind, d].astype(F32) + grecv[layer, kind, d].astype(F32)

    def first_copy(layer, kind, way):
        columns = slice(way * 256, (way + 1) * 256)
        return pltpu.make_async_remote_copy(
            src_ref=first.at[layer, way, kind],
            dst_ref=ring.at[layer, way, 0, kind, :, columns],
            send_sem=first_sem.at[layer, way, kind], recv_sem=ring_recv.at[layer, way, 0, kind],
            device_id=at_dp(sides[way][0]), device_id_type=MESH)

    def ring_copy(layer, kind, way, step):
        return pltpu.make_async_remote_copy(
            src_ref=ring.at[layer, way, step - 1, kind], dst_ref=ring.at[layer, way, step, kind],
            send_sem=ring_send.at[layer, way, step - 1, kind],
            recv_sem=ring_recv.at[layer, way, step, kind],
            device_id=at_dp(sides[way][0]), device_id_type=MESH)

    def ring_first(layer):
        far = lax.rem(me_d + N_DP // 2, N_DP)

        def step(kind, carry):
            pair_copy(layer, kind).wait()
            value = mine(layer, kind, far).astype(BF)
            for way in range(2):
                first[layer, way, kind] = value[:, way * 256:(way + 1) * 256]
                first_copy(layer, kind, way).start()
            return carry
        lax.fori_loop(0, 3, step, 0)

    def ring_step(layer, number):
        def step(kind, carry):
            for way in range(2):
                target = lax.rem(me_d + N_DP + (4 - number) * sides[way][1], N_DP)
                value = mine(layer, kind, target)
                slot = ring.at[layer, way, number - 1, kind]
                if number == 1:
                    first_copy(layer, kind, way).wait()
                    columns = slice(way * 256, (way + 1) * 256)
                    rest = slice((1 - way) * 256, (2 - way) * 256)
                    slot[:, columns] = (slot[:, columns].astype(F32) + value[:, columns]).astype(BF)
                    slot[:, rest] = value[:, rest].astype(BF)
                else:
                    ring_copy(layer, kind, way, number - 1).wait()
                    slot[...] = (slot[...].astype(F32) + value).astype(BF)
                ring_copy(layer, kind, way, number).start()
            return carry
        lax.fori_loop(0, 3, step, 0)

    def ring_last(layer):
        def step(kind, carry):
            value = mine(layer, kind, me_d)
            for way in range(2):
                ring_copy(layer, kind, way, 3).wait()
                value = value + ring[layer, way, 3, kind].astype(F32)
            gsum[layer, kind] = value.astype(BF)
            return carry
        lax.fori_loop(0, 3, step, 0)

    def flat_weights():
        first_row = me_d * PIECE
        offset = lax.rem(first_row, 16)
        rows = pl.ds(pl.multiple_of(first_row - offset, 16), 64)
        for kind in range(3):
            window[...] = w[me_c, kind, rows, :].astype(F32)
            for block in range(16):
                flat_w[pl.ds(kind * 16 + block, PIECE, stride=48), :] = window[
                    pl.ds(pl.multiple_of(offset, 8), PIECE), block * WIDE:(block + 1) * WIDE]

    def flat_sums(source, half):
        for kind in range(3):
            for block in range(8):
                quarter, columns = block // 4, slice(block % 4 * WIDE, (block % 4 + 1) * WIDE)
                value = source[kind, quarter * PIECE:(quarter + 1) * PIECE, columns]
                flat_g[pl.ds(half * 8 + kind * 16 + block, PIECE, stride=48), :] = value.astype(F32)

    for piece in ones:
        piece.finish(1)
    forward(1)
    hidden_grads(1)
    weight_grads_away(1)
    row_grads(1)
    weight_grads_here(1)
    ring_first(1)
    for piece in zeros:
        piece.finish(1)
    forward(0)
    to_tokens(1, dy_ref[me_c])
    upd[...] = (gates[0] * dot(picks[0], dxs[1], 0, 0)).astype(BF)
    launch(grads, (upd[...],))
    ring_step(1, 1)
    for piece in grads:
        piece.send(1)
    flat_weights()
    ring_step(1, 2)
    for piece in grads:
        piece.finish(1)
    hidden_grads(0)
    weight_grads_away(0)
    weight_grads_here(0)
    row_grads(0)
    ring_step(1, 3)
    ring_first(0)
    ring_step(0, 1)
    ring_last(1)
    ring_step(0, 2)
    to_tokens(0, dxs[1])
    dx_copy = to_partner(dxs.at[other], dxoth, dx_sem)
    dx_copy.start()
    ring_step(0, 3)
    for piece in ones + zeros + grads:
        piece.drain()
    dx_copy.wait()
    dx_ref[me_c] = dxs[me_c]
    dx_ref[other] = dxoth[...]
    ring_last(0)
    sum_copy = to_partner(gsum.at[other], goth, gs_sem)
    sum_copy.start()
    flat_sums(gsum.at[me_c], me_c)
    sum_copy.wait()
    flat_sums(goth, other)
    g_ref[...] = flat_g[...].astype(BF)
    w_out_ref[...] = flat_w[...].astype(BF)


def backward(saved, dy, slots, counts, probs, weights):
    dma = pltpu.SemaphoreType.DMA
    vmem, hbm = pl.BlockSpec(memory_space=pltpu.VMEM), pl.BlockSpec(memory_space=pl.ANY)
    scratch = [
        pltpu.VMEM((2, 3, PAD, D), BF),
        pltpu.VMEM((3, TOK, ROWS), BF),
        pltpu.VMEM((3, ROWS, WIDE), F32),
        pltpu.VMEM((3, 2, ROWS, WIDE), BF),
        pltpu.VMEM((2, 2, 4, ROWS, QUAR), BF),
        pltpu.VMEM((ROWS, PAD), F32),
        pltpu.VMEM((ROWS, PAD), F32),
        pltpu.VMEM((ROWS, PAD), BF),
        pltpu.VMEM((ROWS, PAD), BF),
        pltpu.VMEM((ROWS, PAD), BF),
        pltpu.VMEM((3, PAD, ROWS), BF),
        pltpu.VMEM((2, N_TENSOR, ROWS, WIDE), BF),
        pltpu.VMEM((2, N_TENSOR, ROWS, WIDE), BF),
        pltpu.VMEM((2, 3, N_DP, STACK, QUAR), BF),
        pltpu.VMEM((2, 3, N_DP, STACK, QUAR), BF),
        pltpu.VMEM((2, 3, N_DP, STACK, QUAR), BF),
        pltpu.VMEM((2, 2, 3, STACK, QUAR // 2), BF),
        pltpu.VMEM((2, 2, 4, 3, STACK, QUAR), BF),
        pltpu.VMEM((2, 3, STACK, QUAR), BF),
        pltpu.VMEM((3, STACK, QUAR), BF),
        pltpu.VMEM((2, TOK, WIDE), BF),
        pltpu.VMEM((TOK, WIDE), BF),
        pltpu.VMEM((ROWS, WIDE), BF),
        pltpu.VMEM((SHARE // WIDE, WIDE), F32),
        pltpu.VMEM((SHARE // WIDE, WIDE), F32),
        pltpu.VMEM((64, D), F32),
        dma((1,)), dma((2,)), dma((2, 2)), dma((2,)),
        dma((6, 2, 4)), dma((6, 2, 4)), dma((2, N_TENSOR)), dma((2, N_TENSOR)),
        dma((2, 2, 3)), dma((2, 2, 3)), dma((2, 2, 3, 3)), dma((2, 2, 4, 3)), dma((2,)), dma((2,)),
    ]
    return pl.pallas_call(
        kernel,
        out_shape=(jax.ShapeDtypeStruct((2, TOK, WIDE), BF),)
        + (jax.ShapeDtypeStruct((SHARE // WIDE, WIDE), BF),) * 2,
        in_specs=[vmem] * 5 + [hbm],
        out_specs=(vmem,) * 3,
        scratch_shapes=scratch,
        compiler_params=pltpu.CompilerParams(
            collective_id=0, has_side_effects=True, vmem_limit_bytes=60 * 2**20),
        cost_estimate=pl.CostEstimate(
            flops=16 * 2 * ROWS * HID * D, bytes_accessed=30 * 2**20, transcendentals=2 * ROWS * HID),
    )(saved, dy, slots, counts, probs, weights)


def finish(dx_ref, g_ref, w_ref, m_ref, v_ref, dx_out, sum_out, m_out, v_out, w_out):
    @pl.when(pl.program_id(0) == 0)
    def _():
        dx_out[...] = dx_ref[...]

    def step(index, carry):
        span = pl.ds(pl.multiple_of(index * CHUNK, CHUNK), CHUNK)
        lines = CHUNK // WIDE
        rows = pl.ds(pl.multiple_of(index * lines, lines), lines)
        grad = g_ref[rows, :].astype(F32)
        moment_one = m_ref[:, span].reshape(lines, WIDE).astype(F32)
        moment_two = v_ref[:, span].reshape(lines, WIDE).astype(F32)
        moment_one = beta_one * moment_one + (1.0 - beta_one) * grad
        moment_two = beta_two * moment_two + (1.0 - beta_two) * grad * grad
        update = moment_one / bias_one / (jnp.sqrt(moment_two / bias_two) + adam_epsilon)
        fresh = w_ref[rows, :].astype(F32) - learning_rate * update
        sum_out[:, span] = grad.astype(BF).reshape(1, CHUNK)
        m_out[:, span] = moment_one.astype(BF).reshape(1, CHUNK)
        v_out[:, span] = moment_two.astype(BF).reshape(1, CHUNK)
        w_out[:, span] = fresh.astype(BF).reshape(1, CHUNK)
        return carry
    lax.fori_loop(0, SHARE // STEPS // CHUNK, step, 0, unroll=True)


def adam(dx, grad, weights, adam_m, adam_v):
    block = SHARE // STEPS
    whole = pl.BlockSpec((2, TOK, WIDE), lambda i: (0, 0, 0))
    lines = pl.BlockSpec((block // WIDE, WIDE), lambda i: (i, 0))
    flat = pl.BlockSpec((1, block), lambda i: (0, i))
    return pl.pallas_call(
        finish,
        out_shape=(jax.ShapeDtypeStruct(dx.shape, BF),) + (jax.ShapeDtypeStruct((1, SHARE), BF),) * 4,
        grid=(STEPS,),
        in_specs=[whole, lines, lines, flat, flat],
        out_specs=(whole,) + (flat,) * 4,
        compiler_params=pltpu.CompilerParams(vmem_limit_bytes=60 * 2**20),
    )(dx, grad, weights, adam_m, adam_v)


def local(x_saved, dy_in, w_all, slot_token, counts, probs, adam_m, adam_v):
    weights = jnp.transpose(w_all[0], (1, 0, 2))
    results, grad, own = backward(x_saved[0], dy_in, slot_token[0], counts[0].T, probs[0], weights)
    results, sums, new_m, new_v, new_w = adam(results, grad, own, adam_m, adam_v)
    return (results[None], sums, new_m, new_v, new_w)


def solution(mesh):
    return jax.shard_map(
        local,
        mesh=mesh,
        in_specs=(
            P("segment", None, "dp", "tensor"),
            P(None, "dp", "tensor"),
            P("segment", "tensor", None, None),
            P("segment", None, "dp"),
            P("segment", None, "dp"),
            P("segment", None, "dp"),
            P("segment", ("tensor", "dp")),
            P("segment", ("tensor", "dp")),
        ),
        out_specs=(
            P("segment", None, "dp", "tensor"),
            P("segment", ("tensor", "dp")),
            P("segment", ("tensor", "dp")),
            P("segment", ("tensor", "dp")),
            P("segment", ("tensor", "dp")),
        ),
        check_vma=False,
    )
```

```python
import functools

import jax
import jax.numpy as jnp
from jax import lax
from jax.experimental import pallas as pl
from jax.experimental.pallas import tpu as pltpu
from jax.sharding import PartitionSpec as P

beta_one = 0.9
beta_two = 0.95
learning_rate = 0.01
adam_epsilon = 1e-08
bias_one = 0.9999734386011124
bias_two = 0.994079470779666

MESH = pl.DeviceIdType.MESH
BF = jnp.bfloat16
F32 = jnp.float32
N_DP = 8
N_TENSOR = 16
WIDE = 128
D = N_TENSOR * WIDE
ROWS = 256
TOK = 512
HID = 448
PAD = 512
PIECE = HID // N_DP
HALF = D // 2
QUAR = D // 4
STACK = 2 * PIECE
SHARE = 3 * PIECE * D
CHUNK = 8192
STEPS = 6


def dot(left, right, left_dim, right_dim):
    return lax.dot_general(
        left, right, (((left_dim,), (right_dim,)), ((), ())), preferred_element_type=F32
    )


def kernel(x_hbm, dy_hbm, slot_ref, count_ref, prob_ref, w_ref,
           dx_hbm, g_hbm, w_hbm,
           x_ref, dy_ref, dx_ref, g_ref, w_out_ref, w, picks, gates, xr, xd, act, coef, hid, dg, du, trans, back, rs,
           gsend, gown, grecv, first, ring, fin, dxs, dxoth, upd,
           flat_g, flat_w, window, owned, away,
           own_sem, w_sem, pg_sem, xr_sem, ag_send, ag_recv, rs_send, rs_recv,
           gx_sem, first_sem, ring_send, ring_recv, part_sem, dx_sem, fin_sem, in_sem, out_sem):
    me_d, me_t, me_c = lax.axis_index("dp"), lax.axis_index("tensor"), lax.axis_index("segment")
    other = 1 - me_c
    my_y, my_x = me_t // 4, lax.rem(me_t, 4)

    def at_tensor(n):
        return (me_d, n, me_c)

    def at_dp(n):
        return (n, me_t, me_c)

    partner = (me_d, me_t, other)
    up_d, down_d = lax.rem(me_d + 1, N_DP), lax.rem(me_d + N_DP - 1, N_DP)

    def peer(k):
        return ((me_t // 4 + k // 4) % 4) * 4 + (me_t % 4 + k % 4) % 4

    saved_in = pltpu.make_async_copy(x_hbm, x_ref, in_sem.at[0])
    grads_in = pltpu.make_async_copy(dy_hbm, dy_ref, in_sem.at[1])
    saved_in.start()
    grads_in.start()

    barrier = pltpu.get_barrier_semaphore()

    def greet(k, carry):
        pl.semaphore_signal(barrier, inc=1, device_id=at_tensor(peer(k)), device_id_type=MESH)
        return carry
    lax.fori_loop(1, N_TENSOR, greet, 0)
    pl.semaphore_signal(barrier, inc=1, device_id=partner, device_id_type=MESH)
    for layer in range(2):
        pl.semaphore_signal(barrier, inc=1, device_id=(up_d, me_t, layer), device_id_type=MESH)
        pl.semaphore_signal(barrier, inc=1, device_id=(down_d, me_t, layer), device_id_type=MESH)

    own_w = pltpu.make_async_copy(w_ref, w.at[me_c, :, pl.ds(0, HID)], own_sem.at[0])
    own_w.start()
    for layer in range(2):
        for kind in range(3):
            w[layer, kind, HID:PAD, :] = jnp.zeros((PAD - HID, D), BF)
    def rows_of(micro, slot):
        chosen = slot_ref[pl.ds(micro, 1), :]
        tokens = lax.broadcasted_iota(jnp.int32, (TOK, ROWS), 0)
        onehot = jnp.where(tokens == chosen, 1.0, 0.0)
        picks[slot] = onehot.astype(BF)
        both_counts = count_ref[...]
        at_micro = lax.broadcasted_iota(jnp.int32, both_counts.shape, 1) == micro
        count = jnp.sum(jnp.where(at_micro, both_counts, 0), axis=1, keepdims=True)
        live = lax.broadcasted_iota(jnp.int32, (1, ROWS), 1) < count
        gating = jnp.where(live, prob_ref[pl.ds(micro, 1), :], 0.0)
        scale = jnp.broadcast_to(gating, (WIDE, ROWS)).T
        gates[slot] = scale
        both = jnp.concatenate([x_ref[micro], dy_ref[micro]], axis=1)
        picked = dot(picks[slot], both, 0, 0)
        xr[slot, 0] = picked[:, :WIDE].astype(BF)
        xr[slot, 1] = (scale * picked[:, WIDE:]).astype(BF)

    saved_in.wait()
    grads_in.wait()
    rows_of(other, 2)
    rows_of(me_c, me_c)

    pl.semaphore_wait(barrier, N_TENSOR + 4)

    def to_partner(src, dst, sems, index=None):
        send = sems.at[0] if index is None else sems.at[0, index]
        recv = sems.at[1] if index is None else sems.at[1, index]
        return pltpu.make_async_remote_copy(
            src_ref=src, dst_ref=dst, send_sem=send, recv_sem=recv,
            device_id=partner, device_id_type=MESH)

    xr_copy = to_partner(xr.at[2], xr.at[me_c], xr_sem)
    xr_copy.start()
    w_copy = to_partner(w_ref, w.at[me_c, :, pl.ds(0, HID)], w_sem)
    w_copy.start()
    pick_copy = to_partner(picks.at[2], picks.at[me_c], pg_sem, 0)
    pick_copy.start()
    gate_copy = to_partner(gates.at[2], gates.at[me_c], pg_sem, 1)
    gate_copy.start()

    def hop(use, phase, which, ref, device):
        return pltpu.make_async_remote_copy(
            src_ref=ref, dst_ref=ref, send_sem=ag_send.at[use, phase, which],
            recv_sem=ag_recv.at[use, phase, which], device_id=device, device_id_type=MESH)

    class Piece:
        def __init__(self, use, layer, kind, start, rows, x_first, direct):
            self.use, self.layer, self.kind = use, layer, kind
            self.start, self.rows, self.x_first, self.direct = start, rows, x_first, direct

        def at(self, phase, shift):
            if self.x_first == (phase == 0):
                return at_tensor(my_y * 4 + (my_x + shift) % 4)
            return at_tensor((my_y + shift) % 4 * 4 + my_x)

        def block(self, phase, shift, part):
            along_x = self.x_first == (phase == 0)
            low, count = {"all": (0, self.rows), "low": (0, self.rows // 2),
                          "high": (self.rows // 2, self.rows // 2)}[part]
            rows = slice(self.start + low, self.start + low + count)
            index = ((my_x if along_x else my_y) + shift) % 4
            columns = pl.ds(pl.multiple_of((index if along_x else my_x) * WIDE, WIDE), WIDE)
            array = xd.at[self.layer] if self.kind is None else xd.at[self.layer, pl.ds(self.kind, 1)]
            if phase == 0:
                return array.at[:, my_y if along_x else index, rows, columns]
            return array.at[:, :, rows, columns] if along_x else array.at[:, index, rows, :]

        def put(self, values):
            columns = pl.ds(pl.multiple_of(my_x * WIDE, WIDE), WIDE)
            first = 0 if self.kind is None else self.kind
            for index, value in enumerate(values):
                rows = slice(self.start, self.start + self.rows)
                xd[self.layer, first + index, my_y, rows, columns] = value[rows]

        def hops(self, phase):
            own = [(0, 1, "all", 0, 3), (1, 3, "all", 0, 1)]
            if self.direct:
                return own + [(2, 2, "all", 0, 2)], []
            return own, [(2, 1, "low", 3, 2), (3, 3, "high", 1, 2)]

        def copy(self, phase, hop_of, owner):
            which, shift, part, _, _ = hop_of
            return hop(self.use, phase, which, self.block(phase, owner, part), self.at(phase, shift))

        def send(self, phase):
            if phase == 1:
                self.finish(0)
            for one in self.hops(phase)[0]:
                self.copy(phase, one, one[3]).start()

        def forward(self, phase):
            own, later = self.hops(phase)
            for one, two in zip(own, later):
                self.copy(phase, one, one[4]).wait_recv()
                self.copy(phase, two, two[3]).start()

        def finish(self, phase):
            own, later = self.hops(phase)
            for one in later or own:
                self.copy(phase, one, one[4]).wait_recv()

        def drain(self):
            for phase in range(2):
                own, later = self.hops(phase)
                for one in own + later:
                    self.copy(phase, one, one[3]).wait_send()

    part = ROWS // 2

    def pieces_of(use, layer, kind, direct):
        return (Piece(use, layer, kind, 0, part, True, direct),
                Piece(use + 1, layer, kind, part, part, False, direct))

    ones = pieces_of(0, 1, None, True)
    zeros = pieces_of(2, 0, 0, True)
    grads = pieces_of(4, 0, 1, True)

    def launch(pieces, values):
        for piece in pieces:
            piece.put(values)
            piece.send(0)

    xr_copy.wait()
    launch(ones, (xr[1, 0], xr[1, 1]))
    for piece in ones:
        piece.forward(0)
    for piece in ones:
        piece.send(1)
    launch(zeros, (xr[0, 0],))
    for piece in ones:
        piece.forward(1)
    for piece in zeros:
        piece.forward(0)
    for piece in zeros:
        piece.send(1)
    own_w.wait()
    w_copy.wait()
    pick_copy.wait()
    gate_copy.wait()

    def wide_dot(layer, kind, matrix, span):
        total = None
        for y in range(4):
            part = dot(xd[layer, kind, y], w[layer, matrix, span, y * QUAR:(y + 1) * QUAR], 1, 1)
            total = part if total is None else total + part
        return total

    def forward(layer):
        def step(block, carry):
            span = pl.ds(pl.multiple_of(block * 256, 256), 256)
            gate_pre = wide_dot(layer, 0, 0, span)
            up_pre = wide_dot(layer, 0, 1, span)
            sig = 1.0 / (1.0 + jnp.exp(-gate_pre))
            active = gate_pre * sig
            act[:, span] = active
            coef[:, span] = up_pre * sig * (1.0 + gate_pre * (1.0 - sig))
            hid[:, span] = (active * up_pre).astype(BF)
            return carry
        lax.fori_loop(0, PAD // 256, step, 0)

    def hidden_grads(layer):
        def step(block, carry):
            span = pl.ds(pl.multiple_of(block * 256, 256), 256)
            grad = wide_dot(layer, 1, 2, span)
            dg[:, span] = (grad * coef[:, span]).astype(BF)
            du[:, span] = (grad * act[:, span]).astype(BF)
            return carry
        lax.fori_loop(0, PAD // 256, step, 0)

    def scatter_copy(layer, n, owner):
        return pltpu.make_async_remote_copy(
            src_ref=back.at[layer, n], dst_ref=rs.at[layer, owner],
            send_sem=rs_send.at[layer, n], recv_sem=rs_recv.at[layer, owner],
            device_id=at_tensor(n), device_id_type=MESH)

    def row_grads(layer):
        def step(index, carry):
            pair = lax.rem(me_t // 2 + 1 + index, N_TENSOR // 2)
            span = pl.ds(pl.multiple_of(pair * 256, 256), 256)
            term = dot(dg[...], w[layer, 0, :, span], 1, 0)
            term = (term + dot(du[...], w[layer, 1, :, span], 1, 0)).astype(BF)
            for side in range(2):
                n = pair * 2 + side
                back[layer, n] = term[:, side * WIDE:(side + 1) * WIDE]

                @pl.when(n != me_t)
                def _():
                    scatter_copy(layer, n, me_t).start()
            return carry
        lax.fori_loop(0, N_TENSOR // 2, step, 0)

    def summed_rows(layer):
        def step(k, total):
            n = peer(k)
            scatter_copy(layer, n, n).wait_recv()
            scatter_copy(layer, n, me_t).wait_send()
            return total + rs[layer, n].astype(F32)
        return lax.fori_loop(1, N_TENSOR, step, back[layer, me_t].astype(F32))

    def to_tokens(layer, upstream):
        total = summed_rows(layer)
        high = total.astype(BF)
        low = (total - high.astype(F32)).astype(BF)
        spread = dot(picks[layer], high, 1, 0) + dot(picks[layer], low, 1, 0)
        dxs[layer] = (upstream.astype(F32) + spread).astype(BF)

    def weight_half(layer, half, dst, send):
        def step(kind, carry):
            parts = []
            for quarter in range(2):
                parts.append(dot(trans[kind], xd[layer, kind // 2, half * 2 + quarter], 1, 0))
            for d in range(N_DP):
                rows = slice(d * PIECE, (d + 1) * PIECE)
                both = jnp.concatenate([parts[0][rows], parts[1][rows]], axis=0)
                dst[layer, kind, d] = both.astype(BF)
            if send:
                pair_copy(layer, kind).start()
            return carry
        lax.fori_loop(0, 3, step, 0)

    def pair_copy(layer, kind):
        return pltpu.make_async_remote_copy(
            src_ref=gsend.at[layer, kind], dst_ref=grecv.at[layer, kind],
            send_sem=gx_sem.at[0, layer, kind], recv_sem=gx_sem.at[1, layer, kind],
            device_id=partner, device_id_type=MESH)

    def weight_grads_away(layer):
        trans[0] = dg[...].T
        trans[1] = du[...].T
        trans[2] = hid[...].T
        weight_half(layer, other, gsend, True)

    def weight_grads_here(layer):
        weight_half(layer, me_c, gown, False)

    sides = ((up_d, 1), (down_d, -1))

    def mine(layer, kind, d):
        return gown[layer, kind, d].astype(F32) + grecv[layer, kind, d].astype(F32)

    def first_copy(layer, kind, way):
        columns = slice(way * 256, (way + 1) * 256)
        return pltpu.make_async_remote_copy(
            src_ref=first.at[layer, way, kind],
            dst_ref=ring.at[layer, way, 0, kind, :, columns],
            send_sem=first_sem.at[layer, way, kind], recv_sem=ring_recv.at[layer, way, 0, kind],
            device_id=at_dp(sides[way][0]), device_id_type=MESH)

    def ring_copy(layer, kind, way, step):
        return pltpu.make_async_remote_copy(
            src_ref=ring.at[layer, way, step - 1, kind], dst_ref=ring.at[layer, way, step, kind],
            send_sem=ring_send.at[layer, way, step - 1, kind],
            recv_sem=ring_recv.at[layer, way, step, kind],
            device_id=at_dp(sides[way][0]), device_id_type=MESH)

    def ring_first(layer):
        far = lax.rem(me_d + N_DP // 2, N_DP)

        def step(kind, carry):
            pair_copy(layer, kind).wait()
            value = mine(layer, kind, far).astype(BF)
            for way in range(2):
                first[layer, way, kind] = value[:, way * 256:(way + 1) * 256]
                first_copy(layer, kind, way).start()
            return carry
        lax.fori_loop(0, 3, step, 0)

    def ring_step(layer, number):
        def step(kind, carry):
            for way in range(2):
                target = lax.rem(me_d + N_DP + (4 - number) * sides[way][1], N_DP)
                value = mine(layer, kind, target)
                slot = ring.at[layer, way, number - 1, kind]
                if number == 1:
                    first_copy(layer, kind, way).wait()
                    columns = slice(way * 256, (way + 1) * 256)
                    rest = slice((1 - way) * 256, (2 - way) * 256)
                    slot[:, columns] = (slot[:, columns].astype(F32) + value[:, columns]).astype(BF)
                    slot[:, rest] = value[:, rest].astype(BF)
                else:
                    ring_copy(layer, kind, way, number - 1).wait()
                    slot[...] = (slot[...].astype(F32) + value).astype(BF)
                if number < 3:
                    ring_copy(layer, kind, way, number).start()
                else:
                    last_copy(layer, kind, way, me_c).start()
            return carry
        lax.fori_loop(0, 3, step, 0)

    def last_copy(layer, kind, way, half):
        return pltpu.make_async_remote_copy(
            src_ref=ring.at[layer, way, 2, kind], dst_ref=fin.at[half, way, kind],
            send_sem=ring_send.at[layer, way, 2, kind], recv_sem=fin_sem.at[half, way, kind],
            device_id=(sides[way][0], me_t, layer), device_id_type=MESH)

    def own_parts():
        for kind in range(3):
            owned[me_c, kind] = mine(me_c, kind, me_d).astype(BF)
            away[kind] = mine(other, kind, me_d).astype(BF)

    def flat_weights():
        first_row = me_d * PIECE
        offset = lax.rem(first_row, 16)
        rows = pl.ds(pl.multiple_of(first_row - offset, 16), 64)
        for kind in range(3):
            window[...] = w[me_c, kind, rows, :].astype(F32)
            for block in range(16):
                flat_w[pl.ds(kind * 16 + block, PIECE, stride=48), :] = window[
                    pl.ds(pl.multiple_of(offset, 8), PIECE), block * WIDE:(block + 1) * WIDE]

    def flat_sums():
        for kind in range(3):
            for half in range(2):
                value = owned[half, kind].astype(F32)
                for way in range(2):
                    last_copy(0, kind, way, half).wait_recv()
                    value = value + fin[half, way, kind].astype(F32)
                for block in range(8):
                    rows = slice(block // 4 * PIECE, (block // 4 + 1) * PIECE)
                    columns = slice(block % 4 * WIDE, (block % 4 + 1) * WIDE)
                    flat_g[pl.ds(half * 8 + kind * 16 + block, PIECE, stride=48), :] = value[rows, columns]

    for piece in ones:
        piece.finish(1)
    forward(1)
    hidden_grads(1)
    row_grads(1)
    weight_grads_away(1)
    weight_grads_here(1)
    ring_first(1)
    ring_step(1, 1)
    for piece in zeros:
        piece.finish(1)
    forward(0)
    to_tokens(1, dy_ref[me_c])
    upd[...] = (gates[0] * dot(picks[0], dxs[1], 0, 0)).astype(BF)
    launch(grads, (upd[...],))
    ring_step(1, 2)
    for piece in grads:
        piece.send(1)
    flat_weights()
    for piece in grads:
        piece.finish(1)
    ring_step(1, 3)
    hidden_grads(0)
    weight_grads_away(0)
    weight_grads_here(0)
    row_grads(0)
    ring_first(0)
    own_parts()
    part_copy = to_partner(away, owned.at[me_c], part_sem)
    part_copy.start()
    ring_step(0, 1)
    ring_step(0, 2)
    to_tokens(0, dxs[1])
    dx_copy = to_partner(dxs.at[other], dxoth, dx_sem)
    dx_copy.start()
    ring_step(0, 3)
    for piece in ones + zeros + grads:
        piece.drain()
    w_out_ref[...] = flat_w[...].astype(BF)
    own_out = pltpu.make_async_copy(w_out_ref, w_hbm, out_sem.at[0])
    own_out.start()
    dx_copy.wait()
    dx_ref[me_c] = dxs[me_c]
    dx_ref[other] = dxoth[...]
    dx_out = pltpu.make_async_copy(dx_ref, dx_hbm, out_sem.at[1])
    dx_out.start()
    part_copy.wait()
    flat_sums()
    g_ref[...] = flat_g[...].astype(BF)
    g_out = pltpu.make_async_copy(g_ref, g_hbm, out_sem.at[2])
    g_out.start()
    for layer in range(2):
        for kind in range(3):
            for way in range(2):
                last_copy(layer, kind, way, me_c).wait_send()
    own_out.wait()
    dx_out.wait()
    g_out.wait()


def backward(saved, dy, slots, counts, probs, weights):
    dma = pltpu.SemaphoreType.DMA
    vmem, hbm = pl.BlockSpec(memory_space=pltpu.VMEM), pl.BlockSpec(memory_space=pl.ANY)
    scratch = [
        pltpu.VMEM((2, TOK, WIDE), BF),
        pltpu.VMEM((2, TOK, WIDE), BF),
        pltpu.VMEM((2, TOK, WIDE), BF),
        pltpu.VMEM((SHARE // WIDE, WIDE), BF),
        pltpu.VMEM((SHARE // WIDE, WIDE), BF),
        pltpu.VMEM((2, 3, PAD, D), BF),
        pltpu.VMEM((3, TOK, ROWS), BF),
        pltpu.VMEM((3, ROWS, WIDE), F32),
        pltpu.VMEM((3, 2, ROWS, WIDE), BF),
        pltpu.VMEM((2, 2, 4, ROWS, QUAR), BF),
        pltpu.VMEM((ROWS, PAD), F32),
        pltpu.VMEM((ROWS, PAD), F32),
        pltpu.VMEM((ROWS, PAD), BF),
        pltpu.VMEM((ROWS, PAD), BF),
        pltpu.VMEM((ROWS, PAD), BF),
        pltpu.VMEM((3, PAD, ROWS), BF),
        pltpu.VMEM((2, N_TENSOR, ROWS, WIDE), BF),
        pltpu.VMEM((2, N_TENSOR, ROWS, WIDE), BF),
        pltpu.VMEM((2, 3, N_DP, STACK, QUAR), BF),
        pltpu.VMEM((2, 3, N_DP, STACK, QUAR), BF),
        pltpu.VMEM((2, 3, N_DP, STACK, QUAR), BF),
        pltpu.VMEM((2, 2, 3, STACK, QUAR // 2), BF),
        pltpu.VMEM((2, 2, 3, 3, STACK, QUAR), BF),
        pltpu.VMEM((2, 2, 3, STACK, QUAR), BF),
        pltpu.VMEM((2, TOK, WIDE), BF),
        pltpu.VMEM((TOK, WIDE), BF),
        pltpu.VMEM((ROWS, WIDE), BF),
        pltpu.VMEM((SHARE // WIDE, WIDE), F32),
        pltpu.VMEM((SHARE // WIDE, WIDE), F32),
        pltpu.VMEM((64, D), F32),
        pltpu.VMEM((2, 3, STACK, QUAR), BF),
        pltpu.VMEM((3, STACK, QUAR), BF),
        dma((1,)), dma((2,)), dma((2, 2)), dma((2,)),
        dma((6, 2, 4)), dma((6, 2, 4)), dma((2, N_TENSOR)), dma((2, N_TENSOR)),
        dma((2, 2, 3)), dma((2, 2, 3)), dma((2, 2, 3, 3)), dma((2, 2, 3, 3)), dma((2,)), dma((2,)),
        dma((2, 2, 3)), dma((2,)), dma((3,)),
    ]
    return pl.pallas_call(
        kernel,
        out_shape=(jax.ShapeDtypeStruct((2, TOK, WIDE), BF),)
        + (jax.ShapeDtypeStruct((SHARE // WIDE, WIDE), BF),) * 2,
        in_specs=[hbm, hbm, vmem, vmem, vmem, hbm],
        out_specs=(hbm,) * 3,
        scratch_shapes=scratch,
        compiler_params=pltpu.CompilerParams(
            collective_id=0, has_side_effects=True, vmem_limit_bytes=60 * 2**20),
        cost_estimate=pl.CostEstimate(
            flops=16 * 2 * ROWS * HID * D, bytes_accessed=30 * 2**20, transcendentals=2 * ROWS * HID),
    )(saved, dy, slots, counts, probs, weights)


def finish(dx_ref, g_ref, w_ref, m_ref, v_ref, dx_out, sum_out, m_out, v_out, w_out):
    @pl.when(pl.program_id(0) == 0)
    def _():
        dx_out[...] = dx_ref[...]

    def step(index, carry):
        span = pl.ds(pl.multiple_of(index * CHUNK, CHUNK), CHUNK)
        lines = CHUNK // WIDE
        rows = pl.ds(pl.multiple_of(index * lines, lines), lines)
        grad = g_ref[rows, :].astype(F32)
        moment_one = m_ref[:, span].reshape(lines, WIDE).astype(F32)
        moment_two = v_ref[:, span].reshape(lines, WIDE).astype(F32)
        moment_one = beta_one * moment_one + (1.0 - beta_one) * grad
        moment_two = beta_two * moment_two + (1.0 - beta_two) * grad * grad
        update = moment_one / bias_one / (jnp.sqrt(moment_two / bias_two) + adam_epsilon)
        fresh = w_ref[rows, :].astype(F32) - learning_rate * update
        sum_out[:, span] = grad.astype(BF).reshape(1, CHUNK)
        m_out[:, span] = moment_one.astype(BF).reshape(1, CHUNK)
        v_out[:, span] = moment_two.astype(BF).reshape(1, CHUNK)
        w_out[:, span] = fresh.astype(BF).reshape(1, CHUNK)
        return carry
    lax.fori_loop(0, SHARE // STEPS // CHUNK, step, 0, unroll=True)


def adam(dx, grad, weights, adam_m, adam_v):
    block = SHARE // STEPS
    whole = pl.BlockSpec((2, TOK, WIDE), lambda i: (0, 0, 0))
    lines = pl.BlockSpec((block // WIDE, WIDE), lambda i: (i, 0))
    flat = pl.BlockSpec((1, block), lambda i: (0, i))
    return pl.pallas_call(
        finish,
        out_shape=(jax.ShapeDtypeStruct(dx.shape, BF),) + (jax.ShapeDtypeStruct((1, SHARE), BF),) * 4,
        grid=(STEPS,),
        in_specs=[whole, lines, lines, flat, flat],
        out_specs=(whole,) + (flat,) * 4,
        compiler_params=pltpu.CompilerParams(vmem_limit_bytes=60 * 2**20),
    )(dx, grad, weights, adam_m, adam_v)


def local(x_saved, dy_in, w_all, slot_token, counts, probs, adam_m, adam_v):
    weights = jnp.transpose(w_all[0], (1, 0, 2))
    results, grad, own = backward(x_saved[0], dy_in, slot_token[0], counts[0].T, probs[0], weights)
    results, sums, new_m, new_v, new_w = adam(results, grad, own, adam_m, adam_v)
    return (results[None], sums, new_m, new_v, new_w)


def solution(mesh):
    return jax.shard_map(
        local,
        mesh=mesh,
        in_specs=(
            P("segment", None, "dp", "tensor"),
            P(None, "dp", "tensor"),
            P("segment", "tensor", None, None),
            P("segment", None, "dp"),
            P("segment", None, "dp"),
            P("segment", None, "dp"),
            P("segment", ("tensor", "dp")),
            P("segment", ("tensor", "dp")),
        ),
        out_specs=(
            P("segment", None, "dp", "tensor"),
            P("segment", ("tensor", "dp")),
            P("segment", ("tensor", "dp")),
            P("segment", ("tensor", "dp")),
            P("segment", ("tensor", "dp")),
        ),
        check_vma=False,
    )
```

```python
import functools

import jax
import jax.numpy as jnp
from jax import lax
from jax.experimental import pallas as pl
from jax.experimental.pallas import tpu as pltpu
from jax.sharding import PartitionSpec as P

beta_one = 0.9
beta_two = 0.95
learning_rate = 0.01
adam_epsilon = 1e-08
bias_one = 0.9999734386011124
bias_two = 0.994079470779666

MESH = pl.DeviceIdType.MESH
BF = jnp.bfloat16
F32 = jnp.float32
N_DP = 8
N_TENSOR = 16
WIDE = 128
D = N_TENSOR * WIDE
ROWS = 256
TOK = 512
HID = 448
PAD = 512
PIECE = HID // N_DP
HALF = D // 2
QUAR = D // 4
STACK = 2 * PIECE
SHARE = 3 * PIECE * D
CHUNK = 8192
STEPS = 3


def dot(left, right, left_dim, right_dim):
    return lax.dot_general(
        left, right, (((left_dim,), (right_dim,)), ((), ())), preferred_element_type=F32
    )


def kernel(x_hbm, dy_hbm, slot_ref, count_ref, prob_ref, w_ref,
           dx_hbm, g_hbm, w_hbm,
           x_ref, dy_ref, dx_ref, g_ref, w_out_ref, w, picks, gates, xr, xd, act, coef, hid, dg, du, trans, back, rs,
           gsend, gown, grecv, first, ring, fin, dxs, dxoth, upd,
           flat_g, flat_w, window, owned, away,
           own_sem, w_sem, pg_sem, xr_sem, ag_send, ag_recv, rs_send, rs_recv,
           gx_sem, first_sem, ring_send, ring_recv, part_sem, dx_sem, fin_sem, in_sem, out_sem):
    me_d, me_t, me_c = lax.axis_index("dp"), lax.axis_index("tensor"), lax.axis_index("segment")
    other = 1 - me_c
    my_y, my_x = me_t // 4, lax.rem(me_t, 4)

    def at_tensor(n):
        return (me_d, n, me_c)

    def at_dp(n):
        return (n, me_t, me_c)

    partner = (me_d, me_t, other)
    up_d, down_d = lax.rem(me_d + 1, N_DP), lax.rem(me_d + N_DP - 1, N_DP)

    def peer(k):
        return ((me_t // 4 + k // 4) % 4) * 4 + (me_t % 4 + k % 4) % 4

    saved_in = pltpu.make_async_copy(x_hbm, x_ref, in_sem.at[0])
    grads_in = pltpu.make_async_copy(dy_hbm, dy_ref, in_sem.at[1])
    saved_in.start()
    grads_in.start()

    barrier = pltpu.get_barrier_semaphore()

    for shift in range(1, 4):
        pl.semaphore_signal(barrier, inc=1, device_id=at_tensor(peer(shift)), device_id_type=MESH)
        pl.semaphore_signal(barrier, inc=1, device_id=at_tensor(peer(4 * shift)), device_id_type=MESH)
    pl.semaphore_signal(barrier, inc=1, device_id=partner, device_id_type=MESH)
    for layer in range(2):
        pl.semaphore_signal(barrier, inc=1, device_id=(up_d, me_t, layer), device_id_type=MESH)
        pl.semaphore_signal(barrier, inc=1, device_id=(down_d, me_t, layer), device_id_type=MESH)

    own_w = pltpu.make_async_copy(w_ref, w.at[me_c, :, pl.ds(0, HID)], own_sem.at[0])
    own_w.start()
    for layer in range(2):
        for kind in range(3):
            w[layer, kind, HID:PAD, :] = jnp.zeros((PAD - HID, D), BF)
    def rows_of(micro, slot):
        chosen = slot_ref[pl.ds(micro, 1), :]
        tokens = lax.broadcasted_iota(jnp.int32, (TOK, ROWS), 0)
        onehot = jnp.where(tokens == chosen, 1.0, 0.0)
        picks[slot] = onehot.astype(BF)
        both_counts = count_ref[...]
        at_micro = lax.broadcasted_iota(jnp.int32, both_counts.shape, 1) == micro
        count = jnp.sum(jnp.where(at_micro, both_counts, 0), axis=1, keepdims=True)
        live = lax.broadcasted_iota(jnp.int32, (1, ROWS), 1) < count
        gating = jnp.where(live, prob_ref[pl.ds(micro, 1), :], 0.0)
        scale = jnp.broadcast_to(gating, (WIDE, ROWS)).T
        gates[slot] = scale
        both = jnp.concatenate([x_ref[micro], dy_ref[micro]], axis=1)
        picked = dot(picks[slot], both, 0, 0)
        xr[slot, 0] = picked[:, :WIDE].astype(BF)
        xr[slot, 1] = (scale * picked[:, WIDE:]).astype(BF)

    saved_in.wait()
    grads_in.wait()
    rows_of(other, 2)
    rows_of(me_c, me_c)

    pl.semaphore_wait(barrier, 11)

    def to_partner(src, dst, sems, index=None):
        send = sems.at[0] if index is None else sems.at[0, index]
        recv = sems.at[1] if index is None else sems.at[1, index]
        return pltpu.make_async_remote_copy(
            src_ref=src, dst_ref=dst, send_sem=send, recv_sem=recv,
            device_id=partner, device_id_type=MESH)

    xr_copy = to_partner(xr.at[2], xr.at[me_c], xr_sem)
    xr_copy.start()
    w_copy = to_partner(w_ref, w.at[me_c, :, pl.ds(0, HID)], w_sem)
    w_copy.start()
    pick_copy = to_partner(picks.at[2], picks.at[me_c], pg_sem, 0)
    pick_copy.start()
    gate_copy = to_partner(gates.at[2], gates.at[me_c], pg_sem, 1)
    gate_copy.start()

    def hop(use, phase, which, ref, device):
        return pltpu.make_async_remote_copy(
            src_ref=ref, dst_ref=ref, send_sem=ag_send.at[use, phase, which],
            recv_sem=ag_recv.at[use, phase, which], device_id=device, device_id_type=MESH)

    class Piece:
        def __init__(self, use, layer, kind, start, rows, x_first, direct):
            self.use, self.layer, self.kind = use, layer, kind
            self.start, self.rows, self.x_first, self.direct = start, rows, x_first, direct

        def at(self, phase, shift):
            if self.x_first == (phase == 0):
                return at_tensor(my_y * 4 + (my_x + shift) % 4)
            return at_tensor((my_y + shift) % 4 * 4 + my_x)

        def block(self, phase, shift, part):
            along_x = self.x_first == (phase == 0)
            low, count = {"all": (0, self.rows), "low": (0, self.rows // 2),
                          "high": (self.rows // 2, self.rows // 2)}[part]
            rows = slice(self.start + low, self.start + low + count)
            index = ((my_x if along_x else my_y) + shift) % 4
            columns = pl.ds(pl.multiple_of((index if along_x else my_x) * WIDE, WIDE), WIDE)
            array = xd.at[self.layer] if self.kind is None else xd.at[self.layer, pl.ds(self.kind, 1)]
            if phase == 0:
                return array.at[:, my_y if along_x else index, rows, columns]
            return array.at[:, :, rows, columns] if along_x else array.at[:, index, rows, :]

        def put(self, values):
            columns = pl.ds(pl.multiple_of(my_x * WIDE, WIDE), WIDE)
            first = 0 if self.kind is None else self.kind
            for index, value in enumerate(values):
                rows = slice(self.start, self.start + self.rows)
                xd[self.layer, first + index, my_y, rows, columns] = value[rows]

        def hops(self, phase):
            own = [(0, 1, "all", 0, 3), (1, 3, "all", 0, 1)]
            if self.direct:
                return own + [(2, 2, "all", 0, 2)], []
            return own, [(2, 1, "low", 3, 2), (3, 3, "high", 1, 2)]

        def copy(self, phase, hop_of, owner):
            which, shift, part, _, _ = hop_of
            return hop(self.use, phase, which, self.block(phase, owner, part), self.at(phase, shift))

        def send(self, phase):
            if phase == 1:
                self.finish(0)
            for one in self.hops(phase)[0]:
                self.copy(phase, one, one[3]).start()

        def forward(self, phase):
            own, later = self.hops(phase)
            for one, two in zip(own, later):
                self.copy(phase, one, one[4]).wait_recv()
                self.copy(phase, two, two[3]).start()

        def finish(self, phase):
            own, later = self.hops(phase)
            for one in later or own:
                self.copy(phase, one, one[4]).wait_recv()

        def drain(self):
            for phase in range(2):
                own, later = self.hops(phase)
                for one in own + later:
                    self.copy(phase, one, one[3]).wait_send()

    part = ROWS // 2

    def pieces_of(use, layer, kind, direct):
        return (Piece(use, layer, kind, 0, part, True, direct),
                Piece(use + 1, layer, kind, part, part, False, direct))

    ones = pieces_of(0, 1, None, True)
    zeros = pieces_of(2, 0, 0, True)
    grads = pieces_of(4, 0, 1, True)

    def launch(pieces, values):
        for piece in pieces:
            piece.put(values)
            piece.send(0)

    xr_copy.wait()
    launch(ones, (xr[1, 0], xr[1, 1]))
    for piece in ones:
        piece.forward(0)
    for piece in ones:
        piece.send(1)
    launch(zeros, (xr[0, 0],))
    for piece in ones:
        piece.forward(1)
    for piece in zeros:
        piece.forward(0)
    for piece in zeros:
        piece.send(1)
    own_w.wait()
    w_copy.wait()
    pick_copy.wait()
    gate_copy.wait()

    def wide_dot(layer, kind, matrix, span):
        total = None
        for y in range(4):
            part = dot(xd[layer, kind, y], w[layer, matrix, span, y * QUAR:(y + 1) * QUAR], 1, 1)
            total = part if total is None else total + part
        return total

    def forward(layer):
        def step(block, carry):
            span = pl.ds(pl.multiple_of(block * 256, 256), 256)
            gate_pre = wide_dot(layer, 0, 0, span)
            up_pre = wide_dot(layer, 0, 1, span)
            sig = 1.0 / (1.0 + jnp.exp(-gate_pre))
            active = gate_pre * sig
            act[:, span] = active
            coef[:, span] = up_pre * sig * (1.0 + gate_pre * (1.0 - sig))
            hid[:, span] = (active * up_pre).astype(BF)
            return carry
        lax.fori_loop(0, PAD // 256, step, 0)

    def hidden_grads(layer):
        def step(block, carry):
            span = pl.ds(pl.multiple_of(block * 256, 256), 256)
            grad = wide_dot(layer, 1, 2, span)
            dg[:, span] = (grad * coef[:, span]).astype(BF)
            du[:, span] = (grad * act[:, span]).astype(BF)
            return carry
        lax.fori_loop(0, PAD // 256, step, 0)

    def scatter_copy(layer, n, owner):
        return pltpu.make_async_remote_copy(
            src_ref=back.at[layer, n], dst_ref=rs.at[layer, owner],
            send_sem=rs_send.at[layer, n], recv_sem=rs_recv.at[layer, owner],
            device_id=at_tensor(n), device_id_type=MESH)

    def row_grads(layer):
        def step(index, carry):
            pair = lax.rem(me_t // 2 + 1 + index, N_TENSOR // 2)
            span = pl.ds(pl.multiple_of(pair * 256, 256), 256)
            term = dot(dg[...], w[layer, 0, :, span], 1, 0)
            term = (term + dot(du[...], w[layer, 1, :, span], 1, 0)).astype(BF)
            for side in range(2):
                n = pair * 2 + side
                back[layer, n] = term[:, side * WIDE:(side + 1) * WIDE]

                @pl.when(n != me_t)
                def _():
                    scatter_copy(layer, n, me_t).start()
            return carry
        lax.fori_loop(0, N_TENSOR // 2, step, 0)

    def summed_rows(layer):
        def step(k, total):
            n = peer(k)
            scatter_copy(layer, n, n).wait_recv()
            scatter_copy(layer, n, me_t).wait_send()
            return total + rs[layer, n].astype(F32)
        return lax.fori_loop(1, N_TENSOR, step, back[layer, me_t].astype(F32))

    def to_tokens(layer, upstream):
        total = summed_rows(layer)
        high = total.astype(BF)
        low = (total - high.astype(F32)).astype(BF)
        spread = dot(picks[layer], high, 1, 0) + dot(picks[layer], low, 1, 0)
        dxs[layer] = (upstream.astype(F32) + spread).astype(BF)

    def weight_half(layer, half, dst, send):
        def step(kind, carry):
            parts = []
            for quarter in range(2):
                parts.append(dot(trans[kind], xd[layer, kind // 2, half * 2 + quarter], 1, 0))
            for d in range(N_DP):
                rows = slice(d * PIECE, (d + 1) * PIECE)
                both = jnp.concatenate([parts[0][rows], parts[1][rows]], axis=0)
                dst[layer, kind, d] = both.astype(BF)
            if send:
                pair_copy(layer, kind).start()
            return carry
        lax.fori_loop(0, 3, step, 0)

    def pair_copy(layer, kind):
        return pltpu.make_async_remote_copy(
            src_ref=gsend.at[layer, kind], dst_ref=grecv.at[layer, kind],
            send_sem=gx_sem.at[0, layer, kind], recv_sem=gx_sem.at[1, layer, kind],
            device_id=partner, device_id_type=MESH)

    def weight_grads_away(layer):
        trans[0] = dg[...].T
        trans[1] = du[...].T
        trans[2] = hid[...].T
        weight_half(layer, other, gsend, True)

    def weight_grads_here(layer):
        weight_half(layer, me_c, gown, False)

    sides = ((up_d, 1), (down_d, -1))

    def mine(layer, kind, d):
        return gown[layer, kind, d].astype(F32) + grecv[layer, kind, d].astype(F32)

    def first_copy(layer, kind, way):
        columns = slice(way * 256, (way + 1) * 256)
        return pltpu.make_async_remote_copy(
            src_ref=first.at[layer, way, kind],
            dst_ref=ring.at[layer, way, 0, kind, :, columns],
            send_sem=first_sem.at[layer, way, kind], recv_sem=ring_recv.at[layer, way, 0, kind],
            device_id=at_dp(sides[way][0]), device_id_type=MESH)

    def ring_copy(layer, kind, way, step):
        return pltpu.make_async_remote_copy(
            src_ref=ring.at[layer, way, step - 1, kind], dst_ref=ring.at[layer, way, step, kind],
            send_sem=ring_send.at[layer, way, step - 1, kind],
            recv_sem=ring_recv.at[layer, way, step, kind],
            device_id=at_dp(sides[way][0]), device_id_type=MESH)

    def ring_first(layer):
        far = lax.rem(me_d + N_DP // 2, N_DP)

        def step(kind, carry):
            pair_copy(layer, kind).wait()
            value = mine(layer, kind, far).astype(BF)
            for way in range(2):
                first[layer, way, kind] = value[:, way * 256:(way + 1) * 256]
                first_copy(layer, kind, way).start()
            return carry
        lax.fori_loop(0, 3, step, 0)

    def ring_step(layer, number):
        def step(kind, carry):
            for way in range(2):
                target = lax.rem(me_d + N_DP + (4 - number) * sides[way][1], N_DP)
                value = mine(layer, kind, target)
                slot = ring.at[layer, way, number - 1, kind]
                if number == 1:
                    first_copy(layer, kind, way).wait()
                    columns = slice(way * 256, (way + 1) * 256)
                    rest = slice((1 - way) * 256, (2 - way) * 256)
                    slot[:, columns] = (slot[:, columns].astype(F32) + value[:, columns]).astype(BF)
                    slot[:, rest] = value[:, rest].astype(BF)
                else:
                    ring_copy(layer, kind, way, number - 1).wait()
                    slot[...] = (slot[...].astype(F32) + value).astype(BF)
                if number < 3:
                    ring_copy(layer, kind, way, number).start()
                else:
                    last_copy(layer, kind, way, me_c).start()
            return carry
        lax.fori_loop(0, 3, step, 0)

    def last_copy(layer, kind, way, half):
        return pltpu.make_async_remote_copy(
            src_ref=ring.at[layer, way, 2, kind], dst_ref=fin.at[half, way, kind],
            send_sem=ring_send.at[layer, way, 2, kind], recv_sem=fin_sem.at[half, way, kind],
            device_id=(sides[way][0], me_t, layer), device_id_type=MESH)

    def own_parts():
        for kind in range(3):
            owned[me_c, kind] = mine(me_c, kind, me_d).astype(BF)
            away[kind] = mine(other, kind, me_d).astype(BF)

    def flat_weights():
        first_row = me_d * PIECE
        offset = lax.rem(first_row, 16)
        rows = pl.ds(pl.multiple_of(first_row - offset, 16), 64)
        for kind in range(3):
            window[...] = w[me_c, kind, rows, :].astype(F32)
            for block in range(16):
                flat_w[pl.ds(kind * 16 + block, PIECE, stride=48), :] = window[
                    pl.ds(pl.multiple_of(offset, 8), PIECE), block * WIDE:(block + 1) * WIDE]

    def flat_sums():
        for kind in range(3):
            for half in range(2):
                value = owned[half, kind].astype(F32)
                for way in range(2):
                    last_copy(0, kind, way, half).wait_recv()
                    value = value + fin[half, way, kind].astype(F32)
                for block in range(8):
                    rows = slice(block // 4 * PIECE, (block // 4 + 1) * PIECE)
                    columns = slice(block % 4 * WIDE, (block % 4 + 1) * WIDE)
                    flat_g[pl.ds(half * 8 + kind * 16 + block, PIECE, stride=48), :] = value[rows, columns]

    for piece in ones:
        piece.finish(1)
    forward(1)
    hidden_grads(1)
    row_grads(1)
    weight_grads_away(1)
    weight_grads_here(1)
    ring_first(1)
    ring_step(1, 1)
    for piece in zeros:
        piece.finish(1)
    forward(0)
    to_tokens(1, dy_ref[me_c])
    upd[...] = (gates[0] * dot(picks[0], dxs[1], 0, 0)).astype(BF)
    launch(grads, (upd[...],))
    ring_step(1, 2)
    for piece in grads:
        piece.send(1)
    flat_weights()
    for piece in grads:
        piece.finish(1)
    ring_step(1, 3)
    hidden_grads(0)
    weight_grads_away(0)
    weight_grads_here(0)
    row_grads(0)
    ring_first(0)
    own_parts()
    part_copy = to_partner(away, owned.at[me_c], part_sem)
    part_copy.start()
    ring_step(0, 1)
    ring_step(0, 2)
    to_tokens(0, dxs[1])
    dx_copy = to_partner(dxs.at[other], dxoth, dx_sem)
    dx_copy.start()
    ring_step(0, 3)
    for piece in ones + zeros + grads:
        piece.drain()
    w_out_ref[...] = flat_w[...].astype(BF)
    own_out = pltpu.make_async_copy(w_out_ref, w_hbm, out_sem.at[0])
    own_out.start()
    dx_copy.wait()
    dx_ref[me_c] = dxs[me_c]
    dx_ref[other] = dxoth[...]
    dx_out = pltpu.make_async_copy(dx_ref, dx_hbm, out_sem.at[1])
    dx_out.start()
    part_copy.wait()
    flat_sums()
    g_ref[...] = flat_g[...].astype(BF)
    g_out = pltpu.make_async_copy(g_ref, g_hbm, out_sem.at[2])
    g_out.start()
    for layer in range(2):
        for kind in range(3):
            for way in range(2):
                last_copy(layer, kind, way, me_c).wait_send()
    own_out.wait()
    dx_out.wait()
    g_out.wait()


def backward(saved, dy, slots, counts, probs, weights):
    dma = pltpu.SemaphoreType.DMA
    vmem, hbm = pl.BlockSpec(memory_space=pltpu.VMEM), pl.BlockSpec(memory_space=pl.ANY)
    scratch = [
        pltpu.VMEM((2, TOK, WIDE), BF),
        pltpu.VMEM((2, TOK, WIDE), BF),
        pltpu.VMEM((2, TOK, WIDE), BF),
        pltpu.VMEM((SHARE // WIDE, WIDE), BF),
        pltpu.VMEM((SHARE // WIDE, WIDE), BF),
        pltpu.VMEM((2, 3, PAD, D), BF),
        pltpu.VMEM((3, TOK, ROWS), BF),
        pltpu.VMEM((3, ROWS, WIDE), F32),
        pltpu.VMEM((3, 2, ROWS, WIDE), BF),
        pltpu.VMEM((2, 2, 4, ROWS, QUAR), BF),
        pltpu.VMEM((ROWS, PAD), F32),
        pltpu.VMEM((ROWS, PAD), F32),
        pltpu.VMEM((ROWS, PAD), BF),
        pltpu.VMEM((ROWS, PAD), BF),
        pltpu.VMEM((ROWS, PAD), BF),
        pltpu.VMEM((3, PAD, ROWS), BF),
        pltpu.VMEM((2, N_TENSOR, ROWS, WIDE), BF),
        pltpu.VMEM((2, N_TENSOR, ROWS, WIDE), BF),
        pltpu.VMEM((2, 3, N_DP, STACK, QUAR), BF),
        pltpu.VMEM((2, 3, N_DP, STACK, QUAR), BF),
        pltpu.VMEM((2, 3, N_DP, STACK, QUAR), BF),
        pltpu.VMEM((2, 2, 3, STACK, QUAR // 2), BF),
        pltpu.VMEM((2, 2, 3, 3, STACK, QUAR), BF),
        pltpu.VMEM((2, 2, 3, STACK, QUAR), BF),
        pltpu.VMEM((2, TOK, WIDE), BF),
        pltpu.VMEM((TOK, WIDE), BF),
        pltpu.VMEM((ROWS, WIDE), BF),
        pltpu.VMEM((SHARE // WIDE, WIDE), F32),
        pltpu.VMEM((SHARE // WIDE, WIDE), F32),
        pltpu.VMEM((64, D), F32),
        pltpu.VMEM((2, 3, STACK, QUAR), BF),
        pltpu.VMEM((3, STACK, QUAR), BF),
        dma((1,)), dma((2,)), dma((2, 2)), dma((2,)),
        dma((6, 2, 4)), dma((6, 2, 4)), dma((2, N_TENSOR)), dma((2, N_TENSOR)),
        dma((2, 2, 3)), dma((2, 2, 3)), dma((2, 2, 3, 3)), dma((2, 2, 3, 3)), dma((2,)), dma((2,)),
        dma((2, 2, 3)), dma((2,)), dma((3,)),
    ]
    return pl.pallas_call(
        kernel,
        out_shape=(jax.ShapeDtypeStruct((2, TOK, WIDE), BF),)
        + (jax.ShapeDtypeStruct((SHARE // WIDE, WIDE), BF),) * 2,
        in_specs=[hbm, hbm, vmem, vmem, vmem, hbm],
        out_specs=(hbm,) * 3,
        scratch_shapes=scratch,
        compiler_params=pltpu.CompilerParams(
            collective_id=0, has_side_effects=True, vmem_limit_bytes=60 * 2**20),
        cost_estimate=pl.CostEstimate(
            flops=16 * 2 * ROWS * HID * D, bytes_accessed=30 * 2**20, transcendentals=2 * ROWS * HID),
    )(saved, dy, slots, counts, probs, weights)


def finish(dx_ref, g_ref, w_ref, m_ref, v_ref, dx_out, sum_out, m_out, v_out, w_out):
    @pl.when(pl.program_id(0) == 0)
    def _():
        dx_out[...] = dx_ref[...]

    def step(index, carry):
        span = pl.ds(pl.multiple_of(index * CHUNK, CHUNK), CHUNK)
        lines = CHUNK // WIDE
        rows = pl.ds(pl.multiple_of(index * lines, lines), lines)
        grad = g_ref[rows, :].astype(F32)
        moment_one = m_ref[:, span].reshape(lines, WIDE).astype(F32)
        moment_two = v_ref[:, span].reshape(lines, WIDE).astype(F32)
        moment_one = beta_one * moment_one + (1.0 - beta_one) * grad
        moment_two = beta_two * moment_two + (1.0 - beta_two) * grad * grad
        update = moment_one / bias_one / (jnp.sqrt(moment_two / bias_two) + adam_epsilon)
        fresh = w_ref[rows, :].astype(F32) - learning_rate * update
        sum_out[:, span] = grad.astype(BF).reshape(1, CHUNK)
        m_out[:, span] = moment_one.astype(BF).reshape(1, CHUNK)
        v_out[:, span] = moment_two.astype(BF).reshape(1, CHUNK)
        w_out[:, span] = fresh.astype(BF).reshape(1, CHUNK)
        return carry
    lax.fori_loop(0, SHARE // STEPS // CHUNK, step, 0, unroll=True)


def adam(dx, grad, weights, adam_m, adam_v):
    block = SHARE // STEPS
    whole = pl.BlockSpec((2, TOK, WIDE), lambda i: (0, 0, 0))
    lines = pl.BlockSpec((block // WIDE, WIDE), lambda i: (i, 0))
    flat = pl.BlockSpec((1, block), lambda i: (0, i))
    return pl.pallas_call(
        finish,
        out_shape=(jax.ShapeDtypeStruct(dx.shape, BF),) + (jax.ShapeDtypeStruct((1, SHARE), BF),) * 4,
        grid=(STEPS,),
        in_specs=[whole, lines, lines, flat, flat],
        out_specs=(whole,) + (flat,) * 4,
        compiler_params=pltpu.CompilerParams(vmem_limit_bytes=60 * 2**20),
    )(dx, grad, weights, adam_m, adam_v)


def local(x_saved, dy_in, w_all, slot_token, counts, probs, adam_m, adam_v):
    weights = jnp.transpose(w_all[0], (1, 0, 2))
    results, grad, own = backward(x_saved[0], dy_in, slot_token[0], counts[0].T, probs[0], weights)
    results, sums, new_m, new_v, new_w = adam(results, grad, own, adam_m, adam_v)
    return (results[None], sums, new_m, new_v, new_w)


def solution(mesh):
    return jax.shard_map(
        local,
        mesh=mesh,
        in_specs=(
            P("segment", None, "dp", "tensor"),
            P(None, "dp", "tensor"),
            P("segment", "tensor", None, None),
            P("segment", None, "dp"),
            P("segment", None, "dp"),
            P("segment", None, "dp"),
            P("segment", ("tensor", "dp")),
            P("segment", ("tensor", "dp")),
        ),
        out_specs=(
            P("segment", None, "dp", "tensor"),
            P("segment", ("tensor", "dp")),
            P("segment", ("tensor", "dp")),
            P("segment", ("tensor", "dp")),
            P("segment", ("tensor", "dp")),
        ),
        check_vma=False,
    )
```

```python
import functools

import jax
import jax.numpy as jnp
from jax import lax
from jax.experimental import pallas as pl
from jax.experimental.pallas import tpu as pltpu
from jax.sharding import PartitionSpec as P

beta_one = 0.9
beta_two = 0.95
learning_rate = 0.01
adam_epsilon = 1e-08
bias_one = 0.9999734386011124
bias_two = 0.994079470779666

MESH = pl.DeviceIdType.MESH
BF = jnp.bfloat16
F32 = jnp.float32
N_DP = 8
N_TENSOR = 16
WIDE = 128
D = N_TENSOR * WIDE
ROWS = 256
TOK = 512
HID = 448
PAD = 512
PIECE = HID // N_DP
HALF = D // 2
QUAR = D // 4
STACK = 2 * PIECE
SHARE = 3 * PIECE * D
CHUNK = 8192
STEPS = 3


def dot(left, right, left_dim, right_dim):
    return lax.dot_general(
        left, right, (((left_dim,), (right_dim,)), ((), ())), preferred_element_type=F32
    )


def kernel(x_hbm, dy_hbm, slot_ref, count_ref, prob_ref, w_ref,
           dx_hbm, g_hbm, w_hbm,
           x_ref, dy_ref, dx_ref, g_ref, w_out_ref, w, picks, gates, xr, xd, act, coef, hid, dg, du, trans, back, rs,
           gsend, gown, grecv, first, ring, fin, dxs, dxoth, upd,
           flat_g, flat_w, window, owned, away,
           own_sem, w_sem, pg_sem, xr_sem, ag_send, ag_recv, rs_send, rs_recv,
           gx_sem, first_sem, ring_send, ring_recv, part_sem, dx_sem, fin_sem, in_sem, out_sem):
    me_d, me_t, me_c = lax.axis_index("dp"), lax.axis_index("tensor"), lax.axis_index("segment")
    other = 1 - me_c
    my_y, my_x = me_t // 4, lax.rem(me_t, 4)

    def at_tensor(n):
        return (me_d, n, me_c)

    def at_dp(n):
        return (n, me_t, me_c)

    partner = (me_d, me_t, other)
    up_d, down_d = lax.rem(me_d + 1, N_DP), lax.rem(me_d + N_DP - 1, N_DP)

    def peer(k):
        return ((me_t // 4 + k // 4) % 4) * 4 + (me_t % 4 + k % 4) % 4

    saved_in = pltpu.make_async_copy(x_hbm, x_ref, in_sem.at[0])
    grads_in = pltpu.make_async_copy(dy_hbm, dy_ref, in_sem.at[1])
    saved_in.start()
    grads_in.start()

    barrier = pltpu.get_barrier_semaphore()

    for shift in range(1, 4):
        pl.semaphore_signal(barrier, inc=1, device_id=at_tensor(peer(shift)), device_id_type=MESH)
        pl.semaphore_signal(barrier, inc=1, device_id=at_tensor(peer(4 * shift)), device_id_type=MESH)
    pl.semaphore_signal(barrier, inc=1, device_id=partner, device_id_type=MESH)
    for layer in range(2):
        pl.semaphore_signal(barrier, inc=1, device_id=(up_d, me_t, layer), device_id_type=MESH)
        pl.semaphore_signal(barrier, inc=1, device_id=(down_d, me_t, layer), device_id_type=MESH)

    own_w = pltpu.make_async_copy(w_ref, w.at[me_c, :, pl.ds(0, HID)], own_sem.at[0])
    own_w.start()
    for layer in range(2):
        for kind in range(3):
            w[layer, kind, HID:PAD, :] = jnp.zeros((PAD - HID, D), BF)
    def rows_of(micro, slot):
        chosen = slot_ref[pl.ds(micro, 1), :]
        tokens = lax.broadcasted_iota(jnp.int32, (TOK, ROWS), 0)
        onehot = jnp.where(tokens == chosen, 1.0, 0.0)
        picks[slot] = onehot.astype(BF)
        both_counts = count_ref[...]
        at_micro = lax.broadcasted_iota(jnp.int32, both_counts.shape, 1) == micro
        count = jnp.sum(jnp.where(at_micro, both_counts, 0), axis=1, keepdims=True)
        live = lax.broadcasted_iota(jnp.int32, (1, ROWS), 1) < count
        gating = jnp.where(live, prob_ref[pl.ds(micro, 1), :], 0.0)
        scale = jnp.broadcast_to(gating, (WIDE, ROWS)).T
        gates[slot] = scale
        both = jnp.concatenate([x_ref[micro], dy_ref[micro]], axis=1)
        picked = dot(picks[slot], both, 0, 0)
        xr[slot, 0] = picked[:, :WIDE].astype(BF)
        xr[slot, 1] = (scale * picked[:, WIDE:]).astype(BF)

    saved_in.wait()
    grads_in.wait()
    rows_of(other, 2)
    rows_of(me_c, me_c)

    pl.semaphore_wait(barrier, 11)

    def to_partner(src, dst, sems, index=None):
        send = sems.at[0] if index is None else sems.at[0, index]
        recv = sems.at[1] if index is None else sems.at[1, index]
        return pltpu.make_async_remote_copy(
            src_ref=src, dst_ref=dst, send_sem=send, recv_sem=recv,
            device_id=partner, device_id_type=MESH)

    xr_copy = to_partner(xr.at[2], xr.at[me_c], xr_sem)
    xr_copy.start()
    w_copy = to_partner(w_ref, w.at[me_c, :, pl.ds(0, HID)], w_sem)
    w_copy.start()
    pick_copy = to_partner(picks.at[2], picks.at[me_c], pg_sem, 0)
    pick_copy.start()
    gate_copy = to_partner(gates.at[2], gates.at[me_c], pg_sem, 1)
    gate_copy.start()

    def hop(use, phase, which, ref, device):
        return pltpu.make_async_remote_copy(
            src_ref=ref, dst_ref=ref, send_sem=ag_send.at[use, phase, which],
            recv_sem=ag_recv.at[use, phase, which], device_id=device, device_id_type=MESH)

    class Piece:
        def __init__(self, use, layer, kind, start, rows, x_first, direct):
            self.use, self.layer, self.kind = use, layer, kind
            self.start, self.rows, self.x_first, self.direct = start, rows, x_first, direct

        def at(self, phase, shift):
            if self.x_first == (phase == 0):
                return at_tensor(my_y * 4 + (my_x + shift) % 4)
            return at_tensor((my_y + shift) % 4 * 4 + my_x)

        def block(self, phase, shift, part):
            along_x = self.x_first == (phase == 0)
            low, count = {"all": (0, self.rows), "low": (0, self.rows // 2),
                          "high": (self.rows // 2, self.rows // 2)}[part]
            rows = slice(self.start + low, self.start + low + count)
            index = ((my_x if along_x else my_y) + shift) % 4
            columns = pl.ds(pl.multiple_of((index if along_x else my_x) * WIDE, WIDE), WIDE)
            array = xd.at[self.layer] if self.kind is None else xd.at[self.layer, pl.ds(self.kind, 1)]
            if phase == 0:
                return array.at[:, my_y if along_x else index, rows, columns]
            return array.at[:, :, rows, columns] if along_x else array.at[:, index, rows, :]

        def put(self, values):
            columns = pl.ds(pl.multiple_of(my_x * WIDE, WIDE), WIDE)
            first = 0 if self.kind is None else self.kind
            for index, value in enumerate(values):
                rows = slice(self.start, self.start + self.rows)
                xd[self.layer, first + index, my_y, rows, columns] = value[rows]

        def hops(self, phase):
            own = [(0, 1, "all", 0, 3), (1, 3, "all", 0, 1)]
            if self.direct:
                return own + [(2, 2, "all", 0, 2)], []
            return own, [(2, 1, "low", 3, 2), (3, 3, "high", 1, 2)]

        def copy(self, phase, hop_of, owner):
            which, shift, part, _, _ = hop_of
            return hop(self.use, phase, which, self.block(phase, owner, part), self.at(phase, shift))

        def send(self, phase):
            if phase == 1:
                self.finish(0)
            for one in self.hops(phase)[0]:
                self.copy(phase, one, one[3]).start()

        def forward(self, phase):
            own, later = self.hops(phase)
            for one, two in zip(own, later):
                self.copy(phase, one, one[4]).wait_recv()
                self.copy(phase, two, two[3]).start()

        def finish(self, phase):
            own, later = self.hops(phase)
            for one in later or own:
                self.copy(phase, one, one[4]).wait_recv()

        def drain(self):
            for phase in range(2):
                own, later = self.hops(phase)
                for one in own + later:
                    self.copy(phase, one, one[3]).wait_send()

    part = ROWS // 2

    def pieces_of(use, layer, kind, direct):
        return (Piece(use, layer, kind, 0, part, True, direct),
                Piece(use + 1, layer, kind, part, part, False, direct))

    ones = pieces_of(0, 1, None, True)
    zeros = pieces_of(2, 0, 0, True)
    grads = pieces_of(4, 0, 1, True)

    def launch(pieces, values):
        for piece in pieces:
            piece.put(values)
            piece.send(0)

    xr_copy.wait()
    launch(ones, (xr[1, 0], xr[1, 1]))
    for piece in ones:
        piece.forward(0)
    for piece in ones:
        piece.send(1)
    launch(zeros, (xr[0, 0],))
    for piece in ones:
        piece.forward(1)
    for piece in zeros:
        piece.forward(0)
    for piece in zeros:
        piece.send(1)
    own_w.wait()
    w_copy.wait()
    pick_copy.wait()
    gate_copy.wait()

    def wide_dot(layer, kind, matrix, span):
        total = None
        for y in range(4):
            part = dot(xd[layer, kind, y], w[layer, matrix, span, y * QUAR:(y + 1) * QUAR], 1, 1)
            total = part if total is None else total + part
        return total

    def forward(layer):
        def step(block, carry):
            span = pl.ds(pl.multiple_of(block * 256, 256), 256)
            gate_pre = wide_dot(layer, 0, 0, span)
            up_pre = wide_dot(layer, 0, 1, span)
            sig = 1.0 / (1.0 + jnp.exp(-gate_pre))
            active = gate_pre * sig
            act[:, span] = active
            coef[:, span] = up_pre * sig * (1.0 + gate_pre * (1.0 - sig))
            hid[:, span] = (active * up_pre).astype(BF)
            return carry
        lax.fori_loop(0, PAD // 256, step, 0)

    def hidden_grads(layer):
        def step(block, carry):
            span = pl.ds(pl.multiple_of(block * 256, 256), 256)
            grad = wide_dot(layer, 1, 2, span)
            dg[:, span] = (grad * coef[:, span]).astype(BF)
            du[:, span] = (grad * act[:, span]).astype(BF)
            return carry
        lax.fori_loop(0, PAD // 256, step, 0)

    def scatter_copy(layer, n, owner):
        return pltpu.make_async_remote_copy(
            src_ref=back.at[layer, n], dst_ref=rs.at[layer, owner],
            send_sem=rs_send.at[layer, n], recv_sem=rs_recv.at[layer, owner],
            device_id=at_tensor(n), device_id_type=MESH)

    def row_grads(layer):
        def step(index, carry):
            pair = lax.rem(me_t // 2 + 1 + index, N_TENSOR // 2)
            span = pl.ds(pl.multiple_of(pair * 256, 256), 256)
            term = dot(dg[...], w[layer, 0, :, span], 1, 0)
            term = (term + dot(du[...], w[layer, 1, :, span], 1, 0)).astype(BF)
            for side in range(2):
                n = pair * 2 + side
                back[layer, n] = term[:, side * WIDE:(side + 1) * WIDE]

                @pl.when(n != me_t)
                def _():
                    scatter_copy(layer, n, me_t).start()
            return carry
        lax.fori_loop(0, N_TENSOR // 2, step, 0)

    def summed_rows(layer):
        def step(k, total):
            n = peer(k)
            scatter_copy(layer, n, n).wait_recv()
            scatter_copy(layer, n, me_t).wait_send()
            return total + rs[layer, n].astype(F32)
        return lax.fori_loop(1, N_TENSOR, step, back[layer, me_t].astype(F32))

    def to_tokens(layer, upstream):
        total = summed_rows(layer)
        high = total.astype(BF)
        low = (total - high.astype(F32)).astype(BF)
        spread = dot(picks[layer], high, 1, 0) + dot(picks[layer], low, 1, 0)
        dxs[layer] = (upstream.astype(F32) + spread).astype(BF)

    def weight_half(layer, half, dst, send):
        def step(kind, carry):
            parts = []
            for quarter in range(2):
                parts.append(dot(trans[kind], xd[layer, kind // 2, half * 2 + quarter], 1, 0))
            for d in range(N_DP):
                rows = slice(d * PIECE, (d + 1) * PIECE)
                both = jnp.concatenate([parts[0][rows], parts[1][rows]], axis=0)
                dst[layer, kind, d] = both.astype(BF)
            if send:
                pair_copy(layer, kind).start()
            return carry
        lax.fori_loop(0, 3, step, 0)

    def pair_copy(layer, kind):
        return pltpu.make_async_remote_copy(
            src_ref=gsend.at[layer, kind], dst_ref=grecv.at[layer, kind],
            send_sem=gx_sem.at[0, layer, kind], recv_sem=gx_sem.at[1, layer, kind],
            device_id=partner, device_id_type=MESH)

    def weight_grads_away(layer):
        trans[0] = dg[...].T
        trans[1] = du[...].T
        trans[2] = hid[...].T
        weight_half(layer, other, gsend, True)

    def weight_grads_here(layer):
        weight_half(layer, me_c, gown, False)

    sides = ((up_d, 1), (down_d, -1))

    def mine(layer, kind, d):
        return gown[layer, kind, d].astype(F32) + grecv[layer, kind, d].astype(F32)

    def first_copy(layer, kind, way):
        columns = slice(way * 256, (way + 1) * 256)
        return pltpu.make_async_remote_copy(
            src_ref=first.at[layer, way, kind],
            dst_ref=ring.at[layer, way, 0, kind, :, columns],
            send_sem=first_sem.at[layer, way, kind], recv_sem=ring_recv.at[layer, way, 0, kind],
            device_id=at_dp(sides[way][0]), device_id_type=MESH)

    def ring_copy(layer, kind, way, step):
        return pltpu.make_async_remote_copy(
            src_ref=ring.at[layer, way, step - 1, kind], dst_ref=ring.at[layer, way, step, kind],
            send_sem=ring_send.at[layer, way, step - 1, kind],
            recv_sem=ring_recv.at[layer, way, step, kind],
            device_id=at_dp(sides[way][0]), device_id_type=MESH)

    def ring_first(layer):
        far = lax.rem(me_d + N_DP // 2, N_DP)

        def step(kind, carry):
            pair_copy(layer, kind).wait()
            value = mine(layer, kind, far).astype(BF)
            for way in range(2):
                first[layer, way, kind] = value[:, way * 256:(way + 1) * 256]
                first_copy(layer, kind, way).start()
            return carry
        lax.fori_loop(0, 3, step, 0)

    def ring_step(layer, number):
        def step(kind, carry):
            for way in range(2):
                target = lax.rem(me_d + N_DP + (4 - number) * sides[way][1], N_DP)
                value = mine(layer, kind, target)
                slot = ring.at[layer, way, number - 1, kind]
                if number == 1:
                    first_copy(layer, kind, way).wait()
                    columns = slice(way * 256, (way + 1) * 256)
                    rest = slice((1 - way) * 256, (2 - way) * 256)
                    slot[:, columns] = (slot[:, columns].astype(F32) + value[:, columns]).astype(BF)
                    slot[:, rest] = value[:, rest].astype(BF)
                else:
                    ring_copy(layer, kind, way, number - 1).wait()
                    slot[...] = (slot[...].astype(F32) + value).astype(BF)
                if number < 3:
                    ring_copy(layer, kind, way, number).start()
                else:
                    last_copy(layer, kind, way, me_c).start()
            return carry
        lax.fori_loop(0, 3, step, 0)

    def last_copy(layer, kind, way, half):
        return pltpu.make_async_remote_copy(
            src_ref=ring.at[layer, way, 2, kind], dst_ref=fin.at[half, way, kind],
            send_sem=ring_send.at[layer, way, 2, kind], recv_sem=fin_sem.at[half, way, kind],
            device_id=(sides[way][0], me_t, layer), device_id_type=MESH)

    def own_parts():
        for kind in range(3):
            owned[me_c, kind] = mine(me_c, kind, me_d).astype(BF)
            away[kind] = mine(other, kind, me_d).astype(BF)

    def flat_weights():
        first_row = me_d * PIECE
        offset = lax.rem(first_row, 16)
        rows = pl.ds(pl.multiple_of(first_row - offset, 16), 64)
        for kind in range(3):
            window[...] = w[me_c, kind, rows, :].astype(F32)
            for block in range(16):
                flat_w[pl.ds(kind * 16 + block, PIECE, stride=48), :] = window[
                    pl.ds(pl.multiple_of(offset, 8), PIECE), block * WIDE:(block + 1) * WIDE]

    def flat_sums():
        for kind in range(3):
            for half in range(2):
                value = owned[half, kind].astype(F32)
                for way in range(2):
                    last_copy(0, kind, way, half).wait_recv()
                    value = value + fin[half, way, kind].astype(F32)
                for block in range(8):
                    rows = slice(block // 4 * PIECE, (block // 4 + 1) * PIECE)
                    columns = slice(block % 4 * WIDE, (block % 4 + 1) * WIDE)
                    flat_g[pl.ds(half * 8 + kind * 16 + block, PIECE, stride=48), :] = value[rows, columns]

    for piece in ones:
        piece.finish(1)
    forward(1)
    hidden_grads(1)
    row_grads(1)
    weight_grads_away(1)
    weight_grads_here(1)
    ring_first(1)
    ring_step(1, 1)
    for piece in zeros:
        piece.finish(1)
    forward(0)
    to_tokens(1, dy_ref[me_c])
    upd[...] = (gates[0] * dot(picks[0], dxs[1], 0, 0)).astype(BF)
    launch(grads, (upd[...],))
    ring_step(1, 2)
    for piece in grads:
        piece.send(1)
    flat_weights()
    for piece in grads:
        piece.finish(1)
    ring_step(1, 3)
    hidden_grads(0)
    weight_grads_away(0)
    weight_grads_here(0)
    ring_first(0)
    row_grads(0)
    own_parts()
    part_copy = to_partner(away, owned.at[me_c], part_sem)
    part_copy.start()
    ring_step(0, 1)
    ring_step(0, 2)
    ring_step(0, 3)
    to_tokens(0, dxs[1])
    dx_copy = to_partner(dxs.at[other], dxoth, dx_sem)
    dx_copy.start()
    for piece in ones + zeros + grads:
        piece.drain()
    w_out_ref[...] = flat_w[...].astype(BF)
    own_out = pltpu.make_async_copy(w_out_ref, w_hbm, out_sem.at[0])
    own_out.start()
    dx_copy.wait()
    dx_ref[me_c] = dxs[me_c]
    dx_ref[other] = dxoth[...]
    dx_out = pltpu.make_async_copy(dx_ref, dx_hbm, out_sem.at[1])
    dx_out.start()
    part_copy.wait()
    flat_sums()
    g_ref[...] = flat_g[...].astype(BF)
    g_out = pltpu.make_async_copy(g_ref, g_hbm, out_sem.at[2])
    g_out.start()
    for layer in range(2):
        for kind in range(3):
            for way in range(2):
                last_copy(layer, kind, way, me_c).wait_send()
    own_out.wait()
    dx_out.wait()
    g_out.wait()


def backward(saved, dy, slots, counts, probs, weights):
    dma = pltpu.SemaphoreType.DMA
    vmem, hbm = pl.BlockSpec(memory_space=pltpu.VMEM), pl.BlockSpec(memory_space=pl.ANY)
    scratch = [
        pltpu.VMEM((2, TOK, WIDE), BF),
        pltpu.VMEM((2, TOK, WIDE), BF),
        pltpu.VMEM((2, TOK, WIDE), BF),
        pltpu.VMEM((SHARE // WIDE, WIDE), BF),
        pltpu.VMEM((SHARE // WIDE, WIDE), BF),
        pltpu.VMEM((2, 3, PAD, D), BF),
        pltpu.VMEM((3, TOK, ROWS), BF),
        pltpu.VMEM((3, ROWS, WIDE), F32),
        pltpu.VMEM((3, 2, ROWS, WIDE), BF),
        pltpu.VMEM((2, 2, 4, ROWS, QUAR), BF),
        pltpu.VMEM((ROWS, PAD), F32),
        pltpu.VMEM((ROWS, PAD), F32),
        pltpu.VMEM((ROWS, PAD), BF),
        pltpu.VMEM((ROWS, PAD), BF),
        pltpu.VMEM((ROWS, PAD), BF),
        pltpu.VMEM((3, PAD, ROWS), BF),
        pltpu.VMEM((2, N_TENSOR, ROWS, WIDE), BF),
        pltpu.VMEM((2, N_TENSOR, ROWS, WIDE), BF),
        pltpu.VMEM((2, 3, N_DP, STACK, QUAR), BF),
        pltpu.VMEM((2, 3, N_DP, STACK, QUAR), BF),
        pltpu.VMEM((2, 3, N_DP, STACK, QUAR), BF),
        pltpu.VMEM((2, 2, 3, STACK, QUAR // 2), BF),
        pltpu.VMEM((2, 2, 3, 3, STACK, QUAR), BF),
        pltpu.VMEM((2, 2, 3, STACK, QUAR), BF),
        pltpu.VMEM((2, TOK, WIDE), BF),
        pltpu.VMEM((TOK, WIDE), BF),
        pltpu.VMEM((ROWS, WIDE), BF),
        pltpu.VMEM((SHARE // WIDE, WIDE), F32),
        pltpu.VMEM((SHARE // WIDE, WIDE), F32),
        pltpu.VMEM((64, D), F32),
        pltpu.VMEM((2, 3, STACK, QUAR), BF),
        pltpu.VMEM((3, STACK, QUAR), BF),
        dma((1,)), dma((2,)), dma((2, 2)), dma((2,)),
        dma((6, 2, 4)), dma((6, 2, 4)), dma((2, N_TENSOR)), dma((2, N_TENSOR)),
        dma((2, 2, 3)), dma((2, 2, 3)), dma((2, 2, 3, 3)), dma((2, 2, 3, 3)), dma((2,)), dma((2,)),
        dma((2, 2, 3)), dma((2,)), dma((3,)),
    ]
    return pl.pallas_call(
        kernel,
        out_shape=(jax.ShapeDtypeStruct((2, TOK, WIDE), BF),)
        + (jax.ShapeDtypeStruct((SHARE // WIDE, WIDE), BF),) * 2,
        in_specs=[hbm, hbm, vmem, vmem, vmem, hbm],
        out_specs=(hbm,) * 3,
        scratch_shapes=scratch,
        compiler_params=pltpu.CompilerParams(
            collective_id=0, has_side_effects=True, vmem_limit_bytes=60 * 2**20),
        cost_estimate=pl.CostEstimate(
            flops=16 * 2 * ROWS * HID * D, bytes_accessed=30 * 2**20, transcendentals=2 * ROWS * HID),
    )(saved, dy, slots, counts, probs, weights)


def finish(dx_ref, g_ref, w_ref, m_ref, v_ref, dx_out, sum_out, m_out, v_out, w_out):
    @pl.when(pl.program_id(0) == 0)
    def _():
        dx_out[...] = dx_ref[...]

    def step(index, carry):
        span = pl.ds(pl.multiple_of(index * CHUNK, CHUNK), CHUNK)
        lines = CHUNK // WIDE
        rows = pl.ds(pl.multiple_of(index * lines, lines), lines)
        grad = g_ref[rows, :].astype(F32)
        moment_one = m_ref[:, span].reshape(lines, WIDE).astype(F32)
        moment_two = v_ref[:, span].reshape(lines, WIDE).astype(F32)
        moment_one = beta_one * moment_one + (1.0 - beta_one) * grad
        moment_two = beta_two * moment_two + (1.0 - beta_two) * grad * grad
        update = moment_one / bias_one / (jnp.sqrt(moment_two / bias_two) + adam_epsilon)
        fresh = w_ref[rows, :].astype(F32) - learning_rate * update
        sum_out[:, span] = grad.astype(BF).reshape(1, CHUNK)
        m_out[:, span] = moment_one.astype(BF).reshape(1, CHUNK)
        v_out[:, span] = moment_two.astype(BF).reshape(1, CHUNK)
        w_out[:, span] = fresh.astype(BF).reshape(1, CHUNK)
        return carry
    lax.fori_loop(0, SHARE // STEPS // CHUNK, step, 0, unroll=True)


def adam(dx, grad, weights, adam_m, adam_v):
    block = SHARE // STEPS
    whole = pl.BlockSpec((2, TOK, WIDE), lambda i: (0, 0, 0))
    lines = pl.BlockSpec((block // WIDE, WIDE), lambda i: (i, 0))
    flat = pl.BlockSpec((1, block), lambda i: (0, i))
    return pl.pallas_call(
        finish,
        out_shape=(jax.ShapeDtypeStruct(dx.shape, BF),) + (jax.ShapeDtypeStruct((1, SHARE), BF),) * 4,
        grid=(STEPS,),
        in_specs=[whole, lines, lines, flat, flat],
        out_specs=(whole,) + (flat,) * 4,
        compiler_params=pltpu.CompilerParams(vmem_limit_bytes=60 * 2**20),
    )(dx, grad, weights, adam_m, adam_v)


def local(x_saved, dy_in, w_all, slot_token, counts, probs, adam_m, adam_v):
    weights = jnp.transpose(w_all[0], (1, 0, 2))
    results, grad, own = backward(x_saved[0], dy_in, slot_token[0], counts[0].T, probs[0], weights)
    results, sums, new_m, new_v, new_w = adam(results, grad, own, adam_m, adam_v)
    return (results[None], sums, new_m, new_v, new_w)


def solution(mesh):
    return jax.shard_map(
        local,
        mesh=mesh,
        in_specs=(
            P("segment", None, "dp", "tensor"),
            P(None, "dp", "tensor"),
            P("segment", "tensor", None, None),
            P("segment", None, "dp"),
            P("segment", None, "dp"),
            P("segment", None, "dp"),
            P("segment", ("tensor", "dp")),
            P("segment", ("tensor", "dp")),
        ),
        out_specs=(
            P("segment", None, "dp", "tensor"),
            P("segment", ("tensor", "dp")),
            P("segment", ("tensor", "dp")),
            P("segment", ("tensor", "dp")),
            P("segment", ("tensor", "dp")),
        ),
        check_vma=False,
    )
```
